256 devices in a mesh: horiz: 16 (over z, core), lev: 4 (over y), fld: 4 (over x).
Axes of the slice: x: 4, y: 4, z: 8, core: 2. Of those that a mesh axis runs over, the one named last changes fastest.
Arguments:
- adj_out: bfloat16 [8, 64, 2048, 128], P('fld', 'lev', 'horiz'), may hold values from -6 to 6
- interp: bfloat16 [2048, 128, 128], P('horiz'), may hold values from -0.5 to 0.5
- vert_wts: float32 [64, 4], P('lev'), may hold values from -3 to 3
- vert_base: int32 [64], P('lev'), may hold values from -1 to 63, as said below
- dep_tile: int32 [2048], P('horiz'), may hold values from 0 to 2047, as said below
- traj_grad: bfloat16 [2, 8, 64, 2048, 128], P(None, 'fld', 'lev', 'horiz'), may hold values from -0.25 to 0.25
Outputs:
- adj_field: float32 [8, 64, 2048, 128], P('fld', 'lev', 'horiz')
- adj_disp: float32 [2, 2048, 128], P(None, 'horiz')
The draws below stay inside these ranges and needn't reach their ends.
Inputs may be any that keep to these rules, and one draw needn't show every extreme that they name: vert_base[l] is l or l - 1; vert_base[0] is -1 and vert_base[63] is 63. `dep_tile`: tiles form blocks of 128 in order, numbered cyclically. The departure tile (the tile's stencils written as one dense matrix, shared by all levels) of an arrival tile lies in the arrival tile's own block, the next block, the previous one, or the block half the number of blocks away (across the pole). Of one block's arrival tiles at most 32 depart from each of these other blocks (with two blocks: at most 32 from the other block); some block reaches 32 from the next block, some block receives 32 from the previous one, and some block reaches 32 from the block across the pole.
All inputs are finite; a program needn't handle non-finite values.
Results may differ from the reference program's by a relative error of at most 0.0003.
Values sent between devices are 32-bit elements; how exact they have to be, the bound alone decides.
A program may use at most 128 MiB of HBM per device.

```python
import jax
import jax.numpy as jnp
from jax import lax

FLD = 8
LEV = 64
TILE = 128
TILES_DEV = 128
TILES = 2048
CAP = 32


def draw_vert_base(key, part):
    key = jax.random.fold_in(key, 23)
    drop = jax.random.randint(key, (LEV,), 0, 2)
    levels = jnp.arange(LEV, dtype=jnp.int32)
    drop = jnp.where(levels == 0, 1, drop)
    drop = jnp.where(levels == LEV - 1, 0, drop)
    return (levels - drop).astype(jnp.int32)


def draw_dep_tile(key, part):
    key = jax.random.fold_in(key, 11)
    nblock = TILES // TILES_DEV
    keys = jax.random.split(key, 6)
    lowest = max(1, CAP // 4)
    upper = max(lowest, CAP // 2) + 1
    to_next = jax.random.randint(keys[0], (nblock,), lowest, upper)
    to_prev = jax.random.randint(keys[1], (nblock,), lowest, upper)
    to_pole = jax.random.randint(keys[5], (nblock,), lowest, upper)
    chosen = jax.random.randint(keys[2], (), 0, nblock)
    blocks = jnp.arange(nblock, dtype=jnp.int32)
    to_next = jnp.where(blocks == chosen, CAP, to_next)
    to_prev = jnp.where(blocks == (chosen + 2) % nblock, CAP, to_prev)
    to_pole = jnp.where(blocks == (chosen + 1) % nblock, CAP, to_pole)
    to_prev = jnp.where(nblock == 2, 0, to_prev)
    to_pole = jnp.where(nblock == 2, 0, to_pole)
    ranks = jax.vmap(lambda k: jax.random.permutation(k, TILES_DEV))(jax.random.split(keys[3], nblock))
    first = to_next[:, None]
    second = (to_next + to_prev)[:, None]
    third = (to_next + to_prev + to_pole)[:, None]
    step = jnp.where(ranks < first, 1, jnp.where(ranks < second, -1, jnp.where(ranks < third, nblock // 2, 0)))
    target = jnp.remainder(blocks[:, None] + step, nblock)
    inside = jax.random.randint(keys[4], (nblock, TILES_DEV), 0, TILES_DEV)
    return (target * TILES_DEV + inside).reshape(-1).astype(jnp.int32)


def shard_levels(rng, extent, cuts, low, top_value):
    gain, own = 1.0, jax.random.fold_in(rng, 6)
    for position, shards_of in cuts:
        steps = jnp.exp(jax.random.uniform(jax.random.fold_in(own, position), (shards_of,), jnp.float32, low / len(cuts), top_value / len(cuts)))
        gain = gain * jnp.repeat(steps, extent[position] // shards_of).reshape([-1 if axis == position else 1 for axis in range(len(extent))])
    return gain


def centred(stream_key, shape, width, reach, cuts=(), held_as=jnp.bfloat16):
    values = jax.random.normal(stream_key, shape, jnp.float32) * width
    if len(cuts) > 0:
        values = shard_levels(stream_key, shape, cuts, -0.22, 0.18) * values
    return jnp.clip(values, min=-reach, max=reach).astype(held_as)


def setup_inputs(seed: int = 0) -> dict:
    streams_of = jax.random.split(jax.random.key(seed), 7)
    adj_out = centred(streams_of[0], (FLD, LEV, TILES, TILE), 1.0, 6.0, ((0, 4), (1, 4), (2, 16)))
    interp = centred(streams_of[1], (TILES, TILE, TILE), TILE ** -0.5, 0.5, ((0, 16),))
    vert_wts = centred(streams_of[2], (LEV, 4), 0.6, 3.0, ((0, 4),), jnp.float32)
    vert_base = draw_vert_base(jax.random.fold_in(streams_of[6], 71), 0)
    dep_tile = draw_dep_tile(jax.random.fold_in(streams_of[6], 71), 0)
    traj_grad = centred(streams_of[5], (2, FLD, LEV, TILES, TILE), (FLD * LEV) ** -0.5, 0.25, ((1, 4), (2, 4), (3, 16)))
    return {"adj_out": adj_out, "interp": interp, "vert_wts": vert_wts, "vert_base": vert_base, "dep_tile": dep_tile, "traj_grad": traj_grad}


def reference(adj_out, interp, vert_wts, vert_base, dep_tile, traj_grad):
    highest = lax.Precision.HIGHEST
    adjoint = adj_out.astype(jnp.float32)
    horiz = jnp.einsum('fltp,tpq->fltq', adjoint, interp.astype(jnp.float32), precision=highest)
    moved = jax.ops.segment_sum(jnp.moveaxis(horiz, 2, 0), dep_tile, num_segments=TILES)
    levels = jnp.arange(LEV, dtype=jnp.int32)
    taps = vert_base[:, None] - 1 + jnp.arange(4, dtype=jnp.int32)[None, :]
    hits = (levels[:, None, None] == taps[None, :, :]).astype(jnp.float32)
    vertical = jnp.sum(hits * vert_wts[None, :, :], axis=2)
    adj_field = jnp.einsum('ml,tflq->fmtq', vertical, moved, precision=highest)
    adj_disp = jnp.einsum('fltp,cfltp->ctp', adjoint, traj_grad.astype(jnp.float32), precision=highest)
    return adj_field, adj_disp
```

```python
import functools

import jax
import jax.numpy as jnp
from jax import lax
from jax.experimental import pallas as pl
from jax.experimental.pallas import tpu as pltpu
from jax.sharding import PartitionSpec as P

MESH = pl.DeviceIdType.MESH
CAP = 32
ROLES = 3
GROUP = 8
GROUPS = CAP // GROUP
SLOTS = ROLES * CAP
F32, BF16 = jnp.float32, jnp.bfloat16


def split(values):
    high = values.astype(BF16)
    low = (values - high.astype(F32)).astype(BF16)
    return jnp.concatenate([high, low], axis=1)


def spread(hit, values):
    both = jnp.dot(hit, split(values), preferred_element_type=F32)
    width = values.shape[1]
    return both[:, :width] + both[:, width:]


def kernel(
    blocks, levs, flds, nf, nl, tiles,
    adj_hbm, interp_hbm, traj_hbm, dep_ref, wts_ref, base_ref,
    out_hbm, disp_ref,
    adj, interp, traj, adj32, h_slot, h_own, snd, rcv,
    slot_dn, slot_up, slot_dn_in, slot_up_in, own_dn, own_up, own_dn_in, own_up_in,
    acc, label, label_in, index_v, index_s, part, part_x, part_y, whole,
    in_sem, index_sem, out_sem, z_send, z_recv, halo_send, halo_recv, disp_send, disp_recv,
):
    fl = nf * nl
    here, lev, fld = lax.axis_index("horiz"), lax.axis_index("lev"), lax.axis_index("fld")
    core = lax.rem(here, 2)
    pole = lax.rem(here + blocks // 2, blocks)
    across = lax.rem(here + 2 * core - 1 + blocks, blocks)
    mate = here + 1 - 2 * core
    up, down = lax.rem(lev + 1, levs), lax.rem(lev + levs - 1, levs)

    loads = [
        pltpu.make_async_copy(adj_hbm, adj, in_sem.at[0]),
        pltpu.make_async_copy(interp_hbm, interp, in_sem.at[1]),
        pltpu.make_async_copy(traj_hbm, traj, in_sem.at[2]),
    ]
    for load in loads:
        load.start()

    barrier = pltpu.get_barrier_semaphore()
    peers = [{"horiz": pole}, {"horiz": across}, {"horiz": mate}]
    peers += [{"lev": lax.rem(lev + d, levs)} for d in range(1, levs)]
    peers += [{"fld": lax.rem(fld + d, flds)} for d in range(1, flds)]
    for peer in peers:
        pl.semaphore_signal(barrier, inc=1, device_id=peer, device_id_type=MESH)

    square = (tiles, tiles)
    by_lane = jnp.broadcast_to(dep_ref[...], square)
    by_row = by_lane.T
    lane = lax.broadcasted_iota(jnp.int32, square, 1)
    row = lax.broadcasted_iota(jnp.int32, square, 0)

    def role_of(dep):
        owner = dep // tiles
        return jnp.where(owner == pole, 0, jnp.where(owner == across, 1, jnp.where(owner == mate, 2, ROLES)))

    lane_role, row_role = role_of(by_lane), role_of(by_row)
    before = jnp.where((lane_role == row_role) & (row < lane), 1, 0)
    rank = jnp.sum(before, axis=0, keepdims=True)
    slot = jnp.where(lane_role < ROLES, lane_role * CAP + rank, -1)
    chosen = slot.T == lane
    source = jnp.sum(jnp.where(chosen, row, 0), axis=0, keepdims=True)
    target = jnp.sum(jnp.where(chosen, lax.rem(by_row, tiles) + 1, 0), axis=0, keepdims=True) - 1
    index_v[...] = jnp.broadcast_to(source, index_v.shape)
    label[...] = jnp.broadcast_to(target, label.shape)
    index_copy = pltpu.make_async_copy(index_v, index_s, index_sem)
    index_copy.start()
    own_hit = jnp.where((lane_role == ROLES) & (lax.rem(by_lane, tiles) == row), 1.0, 0.0).astype(BF16)

    first = lev * nl
    coef = []
    for l in range(nl):
        late = base_ref[l] < first + l
        taps = [wts_ref[l, j] for j in range(4)]
        coef.append([
            jnp.where(late, taps[k] if k < 4 else 0.0, taps[k - 1] if k > 0 else 0.0) for k in range(5)
        ])

    def vertical(values, emit):
        for e in range(nl + 4):
            total = None
            for l in range(max(0, e - 4), min(nl - 1, e) + 1):
                term = coef[l][e - l] * values[l]
                total = term if total is None else total + term
            emit(e, total)

    loads[0].wait()

    def widen(i, carry):
        adj32[pl.ds(pl.multiple_of(i * tiles, tiles), tiles), :] = adj[i].astype(F32)
        return carry

    lax.fori_loop(0, fl, widen, 0)
    index_copy.wait()
    loads[1].wait()

    def horizontal(t, s, dest, extent):
        rows = [adj32[pl.ds(t + b * 8 * tiles, 8, stride=tiles), :] for b in range(fl // 8)]
        value = jnp.dot(jnp.concatenate(rows, axis=0).astype(BF16), interp[t], preferred_element_type=F32)
        for b in range(fl // 8):
            dest[pl.ds(s + b * 8 * extent, 8, stride=extent), :] = value[b * 8 : b * 8 + 8]

    def work(g):
        at = pl.multiple_of(g * GROUP, GROUP)
        for i in range(GROUP):
            horizontal(index_s[0, at + i], at + i, h_slot, SLOTS)
        for f in range(nf):
            values = [
                h_slot[pl.ds(pl.multiple_of((f * nl + l) * SLOTS + at, GROUP), GROUP), :] for l in range(nl)
            ]

            def emit(e, value, f=f):
                if e < 2:
                    slot_dn[f, e, pl.ds(at, GROUP), :] = value
                elif e < nl + 2:
                    snd[f, e - 2, pl.ds(at, GROUP), :] = value
                else:
                    slot_up[f, e - nl - 2, pl.ds(at, GROUP), :] = value

            vertical(values, emit)

    def inner(g):
        role = g // GROUPS
        partner = jnp.where(role == 0, pole, jnp.where(role == 1, across, mate))
        at = pl.multiple_of(g * GROUP, GROUP)
        piece = (slice(None), pl.ds(2, nl - 4), pl.ds(at, GROUP), slice(None))
        return pltpu.make_async_remote_copy(
            src_ref=snd.at[piece], dst_ref=rcv.at[piece],
            send_sem=z_send.at[g], recv_sem=z_recv.at[g],
            device_id={"horiz": partner}, device_id_type=MESH,
        )

    work(0)
    pl.semaphore_wait(barrier, len(peers))
    inner(0).start()

    def step(g, carry):
        work(g)
        inner(g).start()
        return carry

    lax.fori_loop(1, ROLES * GROUPS, step, 0)

    partners = [pole, across, mate]
    names = [
        pltpu.make_async_remote_copy(
            src_ref=label, dst_ref=label_in.at[r],
            send_sem=z_send.at[ROLES * GROUPS + r], recv_sem=z_recv.at[ROLES * GROUPS + r],
            device_id={"horiz": partners[r]}, device_id_type=MESH,
        )
        for r in range(ROLES)
    ]
    for copy in names:
        copy.start()

    def halo(src, dst, n, target):
        return pltpu.make_async_remote_copy(
            src_ref=src, dst_ref=dst, send_sem=halo_send.at[n], recv_sem=halo_recv.at[n],
            device_id={"lev": target}, device_id_type=MESH,
        )

    slot_halo = [halo(slot_dn, slot_dn_in, 0, down), halo(slot_up, slot_up_in, 1, up)]
    for copy in slot_halo:
        copy.start()

    def own(t, carry):
        horizontal(t, t, h_own, tiles)
        return carry

    lax.fori_loop(0, tiles, own, 0, unroll=8)

    loads[2].wait()

    def displacement(b, carry):
        at = pl.multiple_of(b * 16, 16)
        for c in range(2):
            total = None
            for i in range(fl):
                term = adj32[pl.ds(pl.multiple_of(i * tiles + at, 16), 16), :] * traj[c, i, pl.ds(at, 16), :].astype(F32)
                total = term if total is None else total + term
            part[c, pl.ds(at, 16), :] = total
        return carry

    lax.fori_loop(0, tiles // 16, displacement, 0)
    span = tiles // flds
    short = span // levs

    def disp_copy(src, dst, n, axis, target):
        return pltpu.make_async_remote_copy(
            src_ref=src, dst_ref=dst, send_sem=disp_send.at[n], recv_sem=disp_recv.at[n],
            device_id={axis: target}, device_id_type=MESH,
        )

    to_x = []
    for d in range(1, flds):
        there = lax.rem(fld + d, flds)
        src = part.at[:, pl.ds(pl.multiple_of(there * span, span), span), :]
        to_x.append(disp_copy(src, part_x.at[d - 1], d - 1, "fld", there))
    for copy in to_x:
        copy.start()

    from_below = jnp.where(lev > 0, 1.0, 0.0).astype(F32)
    from_above = jnp.where(lev < levs - 1, 1.0, 0.0).astype(F32)
    for copy in slot_halo:
        copy.wait_recv()

    def edge_levels():
        for e in range(2):
            yield e, slot_up_in, own_up_in, from_below, e
            yield nl - 2 + e, slot_dn_in, own_dn_in, from_above, e

    outer = []
    for f in range(nf):
        for m, slots_in, _, keep, e in edge_levels():
            snd[f, m] = snd[f, m] + keep * slots_in[f, e]
            for r in range(ROLES):
                n = ROLES * GROUPS + ROLES + len(outer)
                piece = (f, m, pl.ds(r * CAP, CAP), slice(None))
                outer.append(pltpu.make_async_remote_copy(
                    src_ref=snd.at[piece], dst_ref=rcv.at[piece],
                    send_sem=z_send.at[n], recv_sem=z_recv.at[n],
                    device_id={"horiz": partners[r]}, device_id_type=MESH,
                ))
                outer[-1].start()

    def gather_own(i, carry):
        at = pl.ds(pl.multiple_of(i * tiles, tiles), tiles)
        h_own[at, :] = spread(own_hit, h_own[at, :])
        return carry

    lax.fori_loop(0, fl, gather_own, 0, unroll=2)

    def own_vertical(b, carry):
        at = pl.multiple_of(b * 8, 8)
        for f in range(nf):
            values = [h_own[pl.ds(pl.multiple_of((f * nl + l) * tiles + at, 8), 8), :] for l in range(nl)]

            def emit(e, value, f=f):
                if e < 2:
                    own_dn[f, e, pl.ds(at, 8), :] = value
                elif e < nl + 2:
                    acc[f, e - 2, pl.ds(at, 8), :] = value
                else:
                    own_up[f, e - nl - 2, pl.ds(at, 8), :] = value

            vertical(values, emit)
        return carry

    lax.fori_loop(0, tiles // 8, own_vertical, 0)
    own_halo = [halo(own_dn, own_dn_in, 2, down), halo(own_up, own_up_in, 3, up)]
    for copy in own_halo:
        copy.start()

    for copy in to_x:
        copy.wait_recv()
    mine = pl.multiple_of(fld * span, span)
    total = part[:, pl.ds(mine, span), :]
    for d in range(flds - 1):
        total = total + part_x[d]
    whole[:, pl.ds(mine, span), :] = total
    to_y = []
    for d in range(1, levs):
        there = lax.rem(lev + d, levs)
        src = whole.at[:, pl.ds(pl.multiple_of(mine + there * short, short), short), :]
        to_y.append(disp_copy(src, part_y.at[d - 1], 3 + d - 1, "lev", there))
    for copy in to_y:
        copy.start()
    for copy in to_y:
        copy.wait()
    piece = pl.multiple_of(mine + lev * short, short)
    total = whole[:, pl.ds(piece, short), :]
    for d in range(levs - 1):
        total = total + part_y[d]
    part[:, pl.ds(piece, short), :] = total
    back_y = []
    for copy in to_x:
        copy.wait_send()
    for d in range(1, levs):
        there = lax.rem(lev + d, levs)
        at = (slice(None), pl.ds(piece, short), slice(None))
        back_y.append(disp_copy(part.at[at], disp_ref.at[at], 6 + d - 1, "lev", there))
    for copy in back_y:
        copy.start()
    disp_ref[:, pl.ds(piece, short), :] = total
    for copy in back_y:
        copy.wait()
    back_x = []
    for d in range(1, flds):
        there = lax.rem(fld + d, flds)
        at = (slice(None), pl.ds(mine, span), slice(None))
        back_x.append(disp_copy(disp_ref.at[at], disp_ref.at[at], 9 + d - 1, "fld", there))
    for copy in back_x:
        copy.start()

    for copy in own_halo:
        copy.wait_recv()
    for f in range(nf):
        for m, _, own_in, keep, e in edge_levels():
            acc[f, m] = acc[f, m] + keep * own_in[f, e]

    for copy in names:
        copy.wait_recv()
    slot_lane = lax.broadcasted_iota(jnp.int32, (1, tiles), 1)
    arrived = jnp.where(slot_lane < CAP, label_in[0, 0:1], jnp.where(slot_lane < 2 * CAP, label_in[1, 0:1], label_in[2, 0:1]))
    arrived = jnp.where(slot_lane < SLOTS, arrived, -1)
    hit = jnp.where(jnp.broadcast_to(arrived, square) == row, 1.0, 0.0).astype(BF16)[:, :SLOTS]

    def store(f, m):
        return pltpu.make_async_copy(acc.at[f, m], out_hbm.at[f, m], out_sem.at[f, m])

    def wait_inner(g, carry):
        inner(g).wait_recv()
        return carry

    lax.fori_loop(0, ROLES * GROUPS, wait_inner, 0)

    def finish(m, carry):
        for f in range(nf):
            acc[f, m] = acc[f, m] + spread(hit, rcv[f, m])
            store(f, m).start()
        return carry

    lax.fori_loop(2, nl - 2, finish, 0)
    n = 0
    for f in range(nf):
        for m, _, _, _, _ in edge_levels():
            for r in range(ROLES):
                outer[n].wait_recv()
                n += 1
            acc[f, m] = acc[f, m] + spread(hit, rcv[f, m])
            store(f, m).start()

    for copy in back_x:
        copy.wait()

    def drain(g, carry):
        inner(g).wait_send()
        return carry

    lax.fori_loop(0, ROLES * GROUPS, drain, 0)
    for copy in outer + names + slot_halo + own_halo:
        copy.wait_send()

    def stored(m, carry):
        for f in range(nf):
            store(f, m).wait()
        return carry

    lax.fori_loop(0, nl, stored, 0)


def shards(mesh, adj_out, interp, vert_wts, vert_base, dep_tile, traj_grad):
    nf, nl, tiles, cols = adj_out.shape
    blocks, levs, flds = mesh.shape["horiz"], mesh.shape["lev"], mesh.shape["fld"]
    fl = nf * nl
    span = tiles // flds
    short = span // levs
    hbm = pl.BlockSpec(memory_space=pl.ANY)
    vmem = pl.BlockSpec(memory_space=pltpu.VMEM)
    smem = pl.BlockSpec(memory_space=pltpu.SMEM)
    n_z = ROLES * GROUPS + ROLES + ROLES * nf * 4
    n_disp = 2 * (flds - 1) + 2 * (levs - 1)
    dma = pltpu.SemaphoreType.DMA
    halo_slots = pltpu.VMEM((nf, 2, SLOTS, cols), F32)
    halo_own = pltpu.VMEM((nf, 2, tiles, cols), F32)
    field, disp = pl.pallas_call(
        functools.partial(kernel, blocks, levs, flds, nf, nl, tiles),
        out_shape=(
            jax.ShapeDtypeStruct((nf, nl, tiles, cols), F32),
            jax.ShapeDtypeStruct((2, tiles, cols), F32),
        ),
        in_specs=[hbm, hbm, hbm, vmem, smem, smem],
        out_specs=(hbm, vmem),
        scratch_shapes=[
            pltpu.VMEM((fl, tiles, cols), BF16),
            pltpu.VMEM((tiles, cols, cols), BF16),
            pltpu.VMEM((2, fl, tiles, cols), BF16),
            pltpu.VMEM((fl * tiles, cols), F32),
            pltpu.VMEM((fl * SLOTS, cols), F32),
            pltpu.VMEM((fl * tiles, cols), F32),
            pltpu.VMEM((nf, nl, SLOTS, cols), F32),
            pltpu.VMEM((nf, nl, SLOTS, cols), F32),
            halo_slots, halo_slots, halo_slots, halo_slots,
            halo_own, halo_own, halo_own, halo_own,
            pltpu.VMEM((nf, nl, tiles, cols), F32),
            pltpu.VMEM((8, tiles), jnp.int32),
            pltpu.VMEM((ROLES, 8, tiles), jnp.int32),
            pltpu.VMEM((8, tiles), jnp.int32),
            pltpu.SMEM((8, tiles), jnp.int32),
            pltpu.VMEM((2, tiles, cols), F32),
            pltpu.VMEM((flds - 1, 2, span, cols), F32),
            pltpu.VMEM((levs - 1, 2, short, cols), F32),
            pltpu.VMEM((2, tiles, cols), F32),
            dma((3,)), dma, dma((nf, nl)), dma((n_z,)), dma((n_z,)),
            dma((4,)), dma((4,)), dma((n_disp,)), dma((n_disp,)),
        ],
        compiler_params=pltpu.CompilerParams(
            collective_id=0, has_side_effects=True, vmem_limit_bytes=48 * 1024 * 1024
        ),
    )(
        adj_out.reshape(fl, tiles, cols), interp, traj_grad.reshape(2, fl, tiles, cols),
        dep_tile.reshape(1, tiles), vert_wts, vert_base,
    )
    return field, disp


def solution(mesh):
    return jax.shard_map(
        functools.partial(shards, mesh),
        mesh=mesh,
        in_specs=(
            P("fld", "lev", "horiz", None),
            P("horiz", None, None),
            P("lev", None),
            P("lev"),
            P("horiz"),
            P(None, "fld", "lev", "horiz", None),
        ),
        out_specs=(P("fld", "lev", "horiz", None), P(None, "horiz", None)),
        check_vma=False,
    )
```

```python
import functools

import jax
import jax.numpy as jnp
from jax import lax
from jax.experimental import pallas as pl
from jax.experimental.pallas import tpu as pltpu
from jax.sharding import PartitionSpec as P

MESH = pl.DeviceIdType.MESH
CAP = 32
ROLES = 3
GROUP = 8
GROUPS = CAP // GROUP
SLOTS = ROLES * CAP
VMEM_BYTES = 48 * 1024 * 1024
F32, BF16 = jnp.float32, jnp.bfloat16


def split(values):
    high = values.astype(BF16)
    low = (values - high.astype(F32)).astype(BF16)
    return jnp.concatenate([high, low], axis=1)


def spread(hit, values):
    both = jnp.dot(hit, split(values), preferred_element_type=F32)
    width = values.shape[1]
    return both[:, :width] + both[:, width:]


def kernel(
    blocks, levs, flds, nf, nl, tiles,
    adj_hbm, interp_hbm, traj_hbm, dep_hbm, wts_hbm, base_hbm,
    acc, disp_ref,
    adj, interp, traj, adj32, h_slot, h_own, snd, rcv,
    slot_dn, slot_up, slot_dn_in, slot_up_in, own_dn, own_up, own_dn_in, own_up_in,
    dep_ref, wts_ref, base_ref, label, label_in, index_v, index_s, part, part_x, part_y, whole,
    in_sem, index_sem, z_send, z_recv, halo_send, halo_recv, disp_send, disp_recv,
):
    fl = nf * nl
    here, lev, fld = lax.axis_index("horiz"), lax.axis_index("lev"), lax.axis_index("fld")
    core = lax.rem(here, 2)
    pole = lax.rem(here + blocks // 2, blocks)
    across = lax.rem(here + 2 * core - 1 + blocks, blocks)
    mate = here + 1 - 2 * core
    up, down = lax.rem(lev + 1, levs), lax.rem(lev + levs - 1, levs)

    pairs = [
        (dep_hbm, dep_ref), (wts_hbm, wts_ref), (base_hbm, base_ref),
        (adj_hbm, adj), (interp_hbm, interp), (traj_hbm, traj),
    ]
    loads = [pltpu.make_async_copy(src, dst, in_sem.at[i]) for i, (src, dst) in enumerate(pairs)]
    for load in loads[:5]:
        load.start()

    barrier = pltpu.get_barrier_semaphore()
    peers = [{"horiz": pole}, {"horiz": across}, {"horiz": mate}]
    peers += [{"lev": lax.rem(lev + d, levs)} for d in range(1, levs)]
    peers += [{"fld": lax.rem(fld + d, flds)} for d in range(1, flds)]
    for peer in peers:
        pl.semaphore_signal(barrier, inc=1, device_id=peer, device_id_type=MESH)

    loads[0].wait()
    square = (tiles, tiles)
    by_lane = jnp.broadcast_to(dep_ref[...], square)
    by_row = by_lane.T
    lane = lax.broadcasted_iota(jnp.int32, square, 1)
    row = lax.broadcasted_iota(jnp.int32, square, 0)

    def role_of(dep):
        owner = dep // tiles
        return jnp.where(owner == pole, 0, jnp.where(owner == across, 1, jnp.where(owner == mate, 2, ROLES)))

    lane_role, row_role = role_of(by_lane), role_of(by_row)
    before = jnp.where((lane_role == row_role) & (row < lane), 1, 0)
    rank = jnp.sum(before, axis=0, keepdims=True)
    slot = jnp.where(lane_role < ROLES, lane_role * CAP + rank, -1)
    chosen = slot.T == lane
    source = jnp.sum(jnp.where(chosen, row, 0), axis=0, keepdims=True)
    target = jnp.sum(jnp.where(chosen, lax.rem(by_row, tiles) + 1, 0), axis=0, keepdims=True) - 1
    index_v[...] = jnp.broadcast_to(source, index_v.shape)
    label[...] = jnp.broadcast_to(target, label.shape)
    index_copy = pltpu.make_async_copy(index_v, index_s, index_sem)
    index_copy.start()
    own_hit = jnp.where((lane_role == ROLES) & (lax.rem(by_lane, tiles) == row), 1.0, 0.0).astype(BF16)

    first = lev * nl
    loads[1].wait()
    loads[2].wait()
    coef = []
    for l in range(nl):
        late = base_ref[l] < first + l
        taps = [wts_ref[j, l] for j in range(4)]
        coef.append([
            jnp.where(late, taps[k] if k < 4 else 0.0, taps[k - 1] if k > 0 else 0.0) for k in range(5)
        ])

    def vertical(values, emit):
        for e in range(nl + 4):
            total = None
            for l in range(max(0, e - 4), min(nl - 1, e) + 1):
                term = coef[l][e - l] * values[l]
                total = term if total is None else total + term
            emit(e, total)

    loads[3].wait()

    def widen(i, carry):
        adj32[pl.ds(pl.multiple_of(i * tiles, tiles), tiles), :] = adj[i].astype(F32)
        return carry

    lax.fori_loop(0, fl, widen, 0)
    index_copy.wait()
    loads[4].wait()
    loads[5].start()

    def horizontal(t, s, dest, extent):
        rows = [adj32[pl.ds(t + b * 8 * tiles, 8, stride=tiles), :] for b in range(fl // 8)]
        value = jnp.dot(jnp.concatenate(rows, axis=0).astype(BF16), interp[t], preferred_element_type=F32)
        for b in range(fl // 8):
            dest[pl.ds(s + b * 8 * extent, 8, stride=extent), :] = value[b * 8 : b * 8 + 8]

    def work(g):
        at = pl.multiple_of(g * GROUP, GROUP)
        for i in range(GROUP):
            horizontal(index_s[0, at + i], at + i, h_slot, SLOTS)
        for f in range(nf):
            values = [
                h_slot[pl.ds(pl.multiple_of((f * nl + l) * SLOTS + at, GROUP), GROUP), :] for l in range(nl)
            ]

            def emit(e, value, f=f):
                if e < 2:
                    slot_dn[f, e, pl.ds(at, GROUP), :] = value
                elif e < nl + 2:
                    snd[f, e - 2, pl.ds(at, GROUP), :] = value
                else:
                    slot_up[f, e - nl - 2, pl.ds(at, GROUP), :] = value

            vertical(values, emit)

    def inner(g):
        role = g // GROUPS
        partner = jnp.where(role == 0, pole, jnp.where(role == 1, across, mate))
        at = pl.multiple_of(g * GROUP, GROUP)
        piece = (slice(None), pl.ds(2, nl - 4), pl.ds(at, GROUP), slice(None))
        return pltpu.make_async_remote_copy(
            src_ref=snd.at[piece], dst_ref=rcv.at[piece],
            send_sem=z_send.at[g], recv_sem=z_recv.at[g],
            device_id={"horiz": partner}, device_id_type=MESH,
        )

    work(0)
    pl.semaphore_wait(barrier, len(peers))
    inner(0).start()

    def step(g, carry):
        work(g)
        inner(g).start()
        return carry

    lax.fori_loop(1, ROLES * GROUPS, step, 0)

    partners = [pole, across, mate]
    names = [
        pltpu.make_async_remote_copy(
            src_ref=label, dst_ref=label_in.at[r],
            send_sem=z_send.at[ROLES * GROUPS + r], recv_sem=z_recv.at[ROLES * GROUPS + r],
            device_id={"horiz": partners[r]}, device_id_type=MESH,
        )
        for r in range(ROLES)
    ]
    for copy in names:
        copy.start()

    def halo(src, dst, n, target):
        return pltpu.make_async_remote_copy(
            src_ref=src, dst_ref=dst, send_sem=halo_send.at[n], recv_sem=halo_recv.at[n],
            device_id={"lev": target}, device_id_type=MESH,
        )

    slot_halo = [halo(slot_dn, slot_dn_in, 0, down), halo(slot_up, slot_up_in, 1, up)]
    for copy in slot_halo:
        copy.start()

    def own(t, carry):
        horizontal(t, t, h_own, tiles)
        return carry

    lax.fori_loop(0, tiles, own, 0, unroll=8)

    loads[5].wait()

    def displacement(b, carry):
        at = pl.multiple_of(b * 16, 16)
        for c in range(2):
            total = None
            for i in range(fl):
                term = adj32[pl.ds(pl.multiple_of(i * tiles + at, 16), 16), :] * traj[c, i, pl.ds(at, 16), :].astype(F32)
                total = term if total is None else total + term
            part[c, pl.ds(at, 16), :] = total
        return carry

    lax.fori_loop(0, tiles // 16, displacement, 0)
    span = tiles // flds
    short = span // levs

    def disp_copy(src, dst, n, axis, target):
        return pltpu.make_async_remote_copy(
            src_ref=src, dst_ref=dst, send_sem=disp_send.at[n], recv_sem=disp_recv.at[n],
            device_id={axis: target}, device_id_type=MESH,
        )

    to_x = []
    for d in range(1, flds):
        there = lax.rem(fld + d, flds)
        src = part.at[:, pl.ds(pl.multiple_of(there * span, span), span), :]
        to_x.append(disp_copy(src, part_x.at[d - 1], d - 1, "fld", there))
    for copy in to_x:
        copy.start()

    from_below = jnp.where(lev > 0, 1.0, 0.0).astype(F32)
    from_above = jnp.where(lev < levs - 1, 1.0, 0.0).astype(F32)
    for copy in slot_halo:
        copy.wait_recv()

    def edge_levels():
        for e in range(2):
            yield e, slot_up_in, own_up_in, from_below, e
            yield nl - 2 + e, slot_dn_in, own_dn_in, from_above, e

    outer = []
    for f in range(nf):
        for m, slots_in, _, keep, e in edge_levels():
            snd[f, m] = snd[f, m] + keep * slots_in[f, e]
            for r in range(ROLES):
                n = ROLES * GROUPS + ROLES + len(outer)
                piece = (f, m, pl.ds(r * CAP, CAP), slice(None))
                outer.append(pltpu.make_async_remote_copy(
                    src_ref=snd.at[piece], dst_ref=rcv.at[piece],
                    send_sem=z_send.at[n], recv_sem=z_recv.at[n],
                    device_id={"horiz": partners[r]}, device_id_type=MESH,
                ))
                outer[-1].start()

    def gather_own(i, carry):
        at = pl.ds(pl.multiple_of(i * tiles, tiles), tiles)
        h_own[at, :] = spread(own_hit, h_own[at, :])
        return carry

    lax.fori_loop(0, fl, gather_own, 0, unroll=2)

    def own_vertical(b, carry):
        at = pl.multiple_of(b * 8, 8)
        for f in range(nf):
            values = [h_own[pl.ds(pl.multiple_of((f * nl + l) * tiles + at, 8), 8), :] for l in range(nl)]

            def emit(e, value, f=f):
                if e < 2:
                    own_dn[f, e, pl.ds(at, 8), :] = value
                elif e < nl + 2:
                    acc[f, e - 2, pl.ds(at, 8), :] = value
                else:
                    own_up[f, e - nl - 2, pl.ds(at, 8), :] = value

            vertical(values, emit)
        return carry

    lax.fori_loop(0, tiles // 8, own_vertical, 0)
    own_halo = [halo(own_dn, own_dn_in, 2, down), halo(own_up, own_up_in, 3, up)]
    for copy in own_halo:
        copy.start()

    for copy in to_x:
        copy.wait_recv()
    mine = pl.multiple_of(fld * span, span)
    total = part[:, pl.ds(mine, span), :]
    for d in range(flds - 1):
        total = total + part_x[d]
    whole[:, pl.ds(mine, span), :] = total
    to_y = []
    for d in range(1, levs):
        there = lax.rem(lev + d, levs)
        src = whole.at[:, pl.ds(pl.multiple_of(mine + there * short, short), short), :]
        to_y.append(disp_copy(src, part_y.at[d - 1], 3 + d - 1, "lev", there))
    for copy in to_y:
        copy.start()
    for copy in to_y:
        copy.wait()
    piece = pl.multiple_of(mine + lev * short, short)
    total = whole[:, pl.ds(piece, short), :]
    for d in range(levs - 1):
        total = total + part_y[d]
    part[:, pl.ds(piece, short), :] = total
    back_y = []
    for copy in to_x:
        copy.wait_send()
    for d in range(1, levs):
        there = lax.rem(lev + d, levs)
        at = (slice(None), pl.ds(piece, short), slice(None))
        back_y.append(disp_copy(part.at[at], disp_ref.at[at], 6 + d - 1, "lev", there))
    for copy in back_y:
        copy.start()
    disp_ref[:, pl.ds(piece, short), :] = total
    for copy in back_y:
        copy.wait()
    back_x = []
    for d in range(1, flds):
        there = lax.rem(fld + d, flds)
        at = (slice(None), pl.ds(mine, span), slice(None))
        back_x.append(disp_copy(disp_ref.at[at], disp_ref.at[at], 9 + d - 1, "fld", there))
    for copy in back_x:
        copy.start()

    for copy in own_halo:
        copy.wait_recv()
    for f in range(nf):
        for m, _, own_in, keep, e in edge_levels():
            acc[f, m] = acc[f, m] + keep * own_in[f, e]

    for copy in names:
        copy.wait_recv()
    slot_lane = lax.broadcasted_iota(jnp.int32, (1, tiles), 1)
    arrived = jnp.where(slot_lane < CAP, label_in[0, 0:1], jnp.where(slot_lane < 2 * CAP, label_in[1, 0:1], label_in[2, 0:1]))
    arrived = jnp.where(slot_lane < SLOTS, arrived, -1)
    hit = jnp.where(jnp.broadcast_to(arrived, square) == row, 1.0, 0.0).astype(BF16)[:, :SLOTS]

    def wait_inner(g, carry):
        inner(g).wait_recv()
        return carry

    lax.fori_loop(0, ROLES * GROUPS, wait_inner, 0)

    def finish(m, carry):
        for f in range(nf):
            acc[f, m] = acc[f, m] + spread(hit, rcv[f, m])
        return carry

    lax.fori_loop(2, nl - 2, finish, 0)
    n = 0
    for f in range(nf):
        for m, _, _, _, _ in edge_levels():
            for r in range(ROLES):
                outer[n].wait_recv()
                n += 1
            acc[f, m] = acc[f, m] + spread(hit, rcv[f, m])

    for copy in back_x:
        copy.wait()

    def drain(g, carry):
        inner(g).wait_send()
        return carry

    lax.fori_loop(0, ROLES * GROUPS, drain, 0)
    for copy in outer + names + slot_halo + own_halo:
        copy.wait_send()


def deliver(field_ref, disp_ref, field_out, disp_out, sem):
    copies = [
        pltpu.make_async_copy(field_ref, field_out, sem.at[0]),
        pltpu.make_async_copy(disp_ref, disp_out, sem.at[1]),
    ]
    for copy in copies:
        copy.start()
    for copy in copies:
        copy.wait()


def shards(mesh, adj_out, interp, vert_wts, vert_base, dep_tile, traj_grad):
    nf, nl, tiles, cols = adj_out.shape
    blocks, levs, flds = mesh.shape["horiz"], mesh.shape["lev"], mesh.shape["fld"]
    fl = nf * nl
    span = tiles // flds
    short = span // levs
    hbm = pl.BlockSpec(memory_space=pl.ANY)
    vmem = pl.BlockSpec(memory_space=pltpu.VMEM)
    n_z = ROLES * GROUPS + ROLES + ROLES * nf * 4
    n_disp = 2 * (flds - 1) + 2 * (levs - 1)
    dma = pltpu.SemaphoreType.DMA
    halo_slots = pltpu.VMEM((nf, 2, SLOTS, cols), F32)
    halo_own = pltpu.VMEM((nf, 2, tiles, cols), F32)
    field, disp = pl.pallas_call(
        functools.partial(kernel, blocks, levs, flds, nf, nl, tiles),
        out_shape=(
            pltpu.VMEM((nf, nl, tiles, cols), F32),
            pltpu.VMEM((2, tiles, cols), F32),
        ),
        in_specs=[hbm] * 6,
        out_specs=(vmem, vmem),
        scratch_shapes=[
            pltpu.VMEM((fl, tiles, cols), BF16),
            pltpu.VMEM((tiles, cols, cols), BF16),
            pltpu.VMEM((2, fl, tiles, cols), BF16),
            pltpu.VMEM((fl * tiles, cols), F32),
            pltpu.VMEM((fl * SLOTS, cols), F32),
            pltpu.VMEM((fl * tiles, cols), F32),
            pltpu.VMEM((nf, nl, SLOTS, cols), F32),
            pltpu.VMEM((nf, nl, SLOTS, cols), F32),
            halo_slots, halo_slots, halo_slots, halo_slots,
            halo_own, halo_own, halo_own, halo_own,
            pltpu.VMEM((1, tiles), jnp.int32),
            pltpu.SMEM((4, nl), F32),
            pltpu.SMEM((nl,), jnp.int32),
            pltpu.VMEM((8, tiles), jnp.int32),
            pltpu.VMEM((ROLES, 8, tiles), jnp.int32),
            pltpu.VMEM((8, tiles), jnp.int32),
            pltpu.SMEM((8, tiles), jnp.int32),
            pltpu.VMEM((2, tiles, cols), F32),
            pltpu.VMEM((flds - 1, 2, span, cols), F32),
            pltpu.VMEM((levs - 1, 2, short, cols), F32),
            pltpu.VMEM((2, tiles, cols), F32),
            dma((6,)), dma, dma((n_z,)), dma((n_z,)),
            dma((4,)), dma((4,)), dma((n_disp,)), dma((n_disp,)),
        ],
        compiler_params=pltpu.CompilerParams(
            collective_id=0, has_side_effects=True, vmem_limit_bytes=VMEM_BYTES
        ),
    )(*[
        pltpu.with_memory_space_constraint(x, pltpu.HBM)
        for x in (
            adj_out.reshape(fl, tiles, cols), interp, traj_grad.reshape(2, fl, tiles, cols),
            dep_tile.reshape(1, tiles), vert_wts.T, vert_base,
        )
    ])
    return pl.pallas_call(
        deliver,
        out_shape=(pltpu.HBM(field.shape, F32), pltpu.HBM(disp.shape, F32)),
        in_specs=[vmem] * 2,
        out_specs=(hbm, hbm),
        scratch_shapes=[dma((2,))],
    )(*[pltpu.with_memory_space_constraint(x, pltpu.VMEM) for x in (field, disp)])


def solution(mesh):
    return jax.shard_map(
        functools.partial(shards, mesh),
        mesh=mesh,
        in_specs=(
            P("fld", "lev", "horiz", None),
            P("horiz", None, None),
            P("lev", None),
            P("lev"),
            P("horiz"),
            P(None, "fld", "lev", "horiz", None),
        ),
        out_specs=(P("fld", "lev", "horiz", None), P(None, "horiz", None)),
        check_vma=False,
    )
```

```python
import functools

import jax
import jax.numpy as jnp
from jax import lax
from jax.experimental import pallas as pl
from jax.experimental.pallas import tpu as pltpu
from jax.sharding import PartitionSpec as P

MESH = pl.DeviceIdType.MESH
CAP = 32
ROLES = 3
GROUP = 8
GROUPS = CAP // GROUP
SLOTS = ROLES * CAP
VMEM_BYTES = 48 * 1024 * 1024
F32, BF16 = jnp.float32, jnp.bfloat16


def split(values):
    high = values.astype(BF16)
    low = (values - high.astype(F32)).astype(BF16)
    return jnp.concatenate([high, low], axis=1)


def spread(hit, values):
    both = jnp.dot(hit, split(values), preferred_element_type=F32)
    width = values.shape[1]
    return both[:, :width] + both[:, width:]


def kernel(
    blocks, levs, flds, nf, nl, tiles,
    adj_hbm, interp_hbm, traj_hbm, dep_hbm, wts_hbm, base_hbm,
    acc, disp_ref,
    adj, interp, traj, adj32, h_slot, h_own, snd, rcv,
    slot_edge, slot_edge_in, own_edge, own_edge_in,
    dep_ref, wts_ref, base_ref, label, label_in, index_v, index_s, part, part_x, part_y, whole,
    in_sem, index_sem, answered, name_sem, z_send, z_recv, halo_send, halo_recv, disp_send, disp_recv,
):
    fl = nf * nl
    here, lev, fld = lax.axis_index("horiz"), lax.axis_index("lev"), lax.axis_index("fld")
    core = lax.rem(here, 2)
    pole = lax.rem(here + blocks // 2, blocks)
    across = lax.rem(here + 2 * core - 1 + blocks, blocks)
    mate = here + 1 - 2 * core
    next_x = lax.rem(fld + 1, flds)
    up, down = lax.rem(lev + 1, levs), lax.rem(lev + levs - 1, levs)

    pairs = [
        (dep_hbm, dep_ref), (wts_hbm, wts_ref), (base_hbm, base_ref),
        (adj_hbm, adj), (interp_hbm, interp), (traj_hbm, traj),
    ]
    loads = [pltpu.make_async_copy(src, dst, in_sem.at[i]) for i, (src, dst) in enumerate(pairs)]
    for load in loads[:5]:
        load.start()

    barrier = pltpu.get_barrier_semaphore()
    partners = [pole, across, mate]
    for partner in partners:
        pl.semaphore_signal(barrier, inc=1, device_id={"horiz": partner}, device_id_type=MESH)
    for axis, me, size in (("lev", lev, levs), ("fld", fld, flds)):
        for d in range(1, size):

            @pl.when(me + d < size)
            def _(axis=axis, me=me, d=d):
                pl.semaphore_signal(barrier, inc=1, device_id={axis: me + d}, device_id_type=MESH)

    loads[0].wait()
    square = (tiles, tiles)
    by_lane = jnp.broadcast_to(dep_ref[...], square)
    by_row = by_lane.T
    lane = lax.broadcasted_iota(jnp.int32, square, 1)
    row = lax.broadcasted_iota(jnp.int32, square, 0)

    def role_of(dep):
        owner = dep // tiles
        return jnp.where(owner == pole, 0, jnp.where(owner == across, 1, jnp.where(owner == mate, 2, ROLES)))

    lane_role, row_role = role_of(by_lane), role_of(by_row)
    before = jnp.where((lane_role == row_role) & (row < lane), 1, 0)
    rank = jnp.sum(before, axis=0, keepdims=True)
    slot = jnp.where(lane_role < ROLES, lane_role * CAP + rank, -1)
    chosen = slot.T == lane
    source = jnp.sum(jnp.where(chosen, row, 0), axis=0, keepdims=True)
    target = jnp.sum(jnp.where(chosen, lax.rem(by_row, tiles) + 1, 0), axis=0, keepdims=True) - 1
    index_v[...] = jnp.broadcast_to(source, index_v.shape)
    for r in range(ROLES):
        label[r] = jnp.broadcast_to(target, label.shape[1:])
    index_copy = pltpu.make_async_copy(index_v, index_s, index_sem)
    index_copy.start()
    own_hit = jnp.where((lane_role == ROLES) & (lax.rem(by_lane, tiles) == row), 1.0, 0.0).astype(BF16)

    first = lev * nl
    loads[1].wait()
    loads[2].wait()
    coef = []
    for l in range(nl):
        late = base_ref[l] < first + l
        taps = [wts_ref[j, l] for j in range(4)]
        coef.append([
            jnp.where(late, taps[k] if k < 4 else 0.0, taps[k - 1] if k > 0 else 0.0) for k in range(5)
        ])

    def vertical(values, emit):
        for e in range(nl + 4):
            total = None
            for l in range(max(0, e - 4), min(nl - 1, e) + 1):
                term = coef[l][e - l] * values[l]
                total = term if total is None else total + term
            emit(e, total)

    loads[3].wait()

    def widen(i, carry):
        adj32[pl.ds(pl.multiple_of(i * tiles, tiles), tiles), :] = adj[i].astype(F32)
        return carry

    lax.fori_loop(0, fl, widen, 0)
    index_copy.wait()
    loads[4].wait()
    loads[5].start()

    def horizontal(t, s, dest, extent):
        rows = [adj32[pl.ds(t + b * 8 * tiles, 8, stride=tiles), :] for b in range(fl // 8)]
        value = jnp.dot(jnp.concatenate(rows, axis=0).astype(BF16), interp[t], preferred_element_type=F32)
        for b in range(fl // 8):
            dest[pl.ds(s + b * 8 * extent, 8, stride=extent), :] = value[b * 8 : b * 8 + 8]

    def work(g):
        at = pl.multiple_of(g * GROUP, GROUP)
        for i in range(GROUP):
            horizontal(index_s[0, at + i], at + i, h_slot, SLOTS)
        for f in range(nf):
            values = [
                h_slot[pl.ds(pl.multiple_of((f * nl + l) * SLOTS + at, GROUP), GROUP), :] for l in range(nl)
            ]

            def emit(e, value, f=f):
                if e < 2:
                    slot_edge[0, f, e, pl.ds(at, GROUP), :] = value
                elif e < nl + 2:
                    snd[f, e - 2, pl.ds(at, GROUP), :] = value
                else:
                    slot_edge[1, f, e - nl - 2, pl.ds(at, GROUP), :] = value

            vertical(values, emit)

    def inner(g):
        role = g // GROUPS
        partner = jnp.where(role == 0, pole, jnp.where(role == 1, across, mate))
        at = pl.multiple_of(g * GROUP, GROUP)
        piece = (slice(None), pl.ds(2, nl - 4), pl.ds(at, GROUP), slice(None))
        return pltpu.make_async_remote_copy(
            src_ref=snd.at[piece], dst_ref=rcv.at[piece],
            send_sem=z_send, recv_sem=z_recv.at[0],
            device_id={"horiz": partner}, device_id_type=MESH,
        )

    work(0)
    pl.semaphore_wait(barrier, ROLES + lev + fld)
    inner(0).start()
    for axis, me, size in (("lev", lev, levs), ("fld", fld, flds)):
        for d in range(1, size):

            @pl.when(me >= d)
            def _(axis=axis, me=me, d=d):
                pl.semaphore_signal(answered, inc=1, device_id={axis: me - d}, device_id_type=MESH)


    def step(g, carry):
        work(g)
        inner(g).start()
        return carry

    lax.fori_loop(1, GROUPS, step, 0)

    loads[5].wait()

    def displacement(b, carry):
        at = pl.multiple_of(b * 16, 16)
        for c in range(2):
            total = None
            for i in range(fl):
                term = adj32[pl.ds(pl.multiple_of(i * tiles + at, 16), 16), :] * traj[c, i, pl.ds(at, 16), :].astype(F32)
                total = term if total is None else total + term
            part[c, pl.ds(at, 16), :] = total
        return carry

    lax.fori_loop(0, tiles // 16, displacement, 0)
    span = tiles // flds
    short = span // levs

    def disp_copy(src, dst, n, axis, target):
        return pltpu.make_async_remote_copy(
            src_ref=src, dst_ref=dst, send_sem=disp_send.at[n], recv_sem=disp_recv.at[n],
            device_id={axis: target}, device_id_type=MESH,
        )

    def disp_all(like, n, axis):
        return disp_copy(like, like, n, axis, next_x if axis == "fld" else up)

    to_x = []
    for d in range(1, flds):
        there = lax.rem(fld + d, flds)
        src = part.at[:, pl.ds(pl.multiple_of(there * span, span), span), :]
        to_x.append(disp_copy(src, part_x.at[d - 1], 0, "fld", there))
    answers = levs - 1 - lev + flds - 1 - fld

    @pl.when(answers > 0)
    def _():
        pl.semaphore_wait(answered, answers)

    for copy in to_x:
        copy.start()

    lax.fori_loop(GROUPS, ROLES * GROUPS, step, 0)

    names = [
        pltpu.make_async_remote_copy(
            src_ref=label.at[r], dst_ref=label_in.at[r], send_sem=name_sem.at[0], recv_sem=name_sem.at[1],
            device_id={"horiz": partners[r]}, device_id_type=MESH,
        )
        for r in range(ROLES)
    ]
    for copy in names:
        copy.start()

    def halo(src, dst, n):
        return [
            pltpu.make_async_remote_copy(
                src_ref=src.at[way], dst_ref=dst.at[way], send_sem=halo_send.at[n], recv_sem=halo_recv.at[n],
                device_id={"lev": target}, device_id_type=MESH,
            )
            for way, target in enumerate((down, up))
        ]

    def halo_both(src, dst, n):
        return pltpu.make_async_remote_copy(
            src_ref=src, dst_ref=dst, send_sem=halo_send.at[n], recv_sem=halo_recv.at[n],
            device_id={"lev": up}, device_id_type=MESH,
        )

    slot_halo = halo(slot_edge, slot_edge_in, 0)
    for copy in slot_halo:
        copy.start()

    disp_all(part_x, 0, "fld").wait_recv()
    mine = pl.multiple_of(fld * span, span)
    total = part[:, pl.ds(mine, span), :]
    for d in range(flds - 1):
        total = total + part_x[d]
    whole[:, pl.ds(mine, span), :] = total
    to_y = []
    for d in range(1, levs):
        there = lax.rem(lev + d, levs)
        src = whole.at[:, pl.ds(pl.multiple_of(mine + there * short, short), short), :]
        to_y.append(disp_copy(src, part_y.at[d - 1], 1, "lev", there))
    for copy in to_y:
        copy.start()

    def own(t, carry):
        horizontal(t, t, h_own, tiles)
        return carry

    lax.fori_loop(0, tiles // 2, own, 0, unroll=8)

    disp_all(part_y, 1, "lev").wait()
    piece = pl.multiple_of(mine + lev * short, short)
    total = whole[:, pl.ds(piece, short), :]
    for d in range(levs - 1):
        total = total + part_y[d]
    part[:, pl.ds(piece, short), :] = total
    back_y = []
    disp_all(part_x, 0, "fld").wait_send()
    for d in range(1, levs):
        there = lax.rem(lev + d, levs)
        at = (slice(None), pl.ds(piece, short), slice(None))
        back_y.append(disp_copy(part.at[at], disp_ref.at[at], 2, "lev", there))
    for copy in back_y:
        copy.start()
    disp_ref[:, pl.ds(piece, short), :] = total

    lax.fori_loop(tiles // 2, tiles, own, 0, unroll=8)

    disp_all(part_y, 2, "lev").wait()
    back_x = []
    for d in range(1, flds):
        there = lax.rem(fld + d, flds)
        at = (slice(None), pl.ds(mine, span), slice(None))
        back_x.append(disp_copy(disp_ref.at[at], disp_ref.at[at], 3, "fld", there))
    for copy in back_x:
        copy.start()


    from_below = jnp.where(lev > 0, 1.0, 0.0).astype(F32)
    from_above = jnp.where(lev < levs - 1, 1.0, 0.0).astype(F32)
    halo_both(slot_edge, slot_edge_in, 0).wait_recv()

    edges = ((0, 1, from_below), (nl - 2, 0, from_above))

    def outer(f, low, r):
        n = 1 + f * 2 + (0 if low == 0 else 1)
        piece = (f, pl.ds(low, 2), pl.ds(r * CAP, CAP), slice(None))
        return pltpu.make_async_remote_copy(
            src_ref=snd.at[piece], dst_ref=rcv.at[piece],
            send_sem=z_send, recv_sem=z_recv.at[n],
            device_id={"horiz": partners[r]}, device_id_type=MESH,
        )

    for f in range(nf):
        for low, way, keep in edges:
            for e in range(2):
                snd[f, low + e] = snd[f, low + e] + keep * slot_edge_in[way, f, e]
            for r in range(ROLES):
                outer(f, low, r).start()

    def gather_own(i, carry):
        at = pl.ds(pl.multiple_of(i * tiles, tiles), tiles)
        h_own[at, :] = spread(own_hit, h_own[at, :])
        return carry

    lax.fori_loop(0, fl, gather_own, 0, unroll=2)

    def own_vertical(b, carry):
        at = pl.multiple_of(b * 8, 8)
        for f in range(nf):
            values = [h_own[pl.ds(pl.multiple_of((f * nl + l) * tiles + at, 8), 8), :] for l in range(nl)]

            def emit(e, value, f=f):
                if e < 2:
                    own_edge[0, f, e, pl.ds(at, 8), :] = value
                elif e < nl + 2:
                    acc[f, e - 2, pl.ds(at, 8), :] = value
                else:
                    own_edge[1, f, e - nl - 2, pl.ds(at, 8), :] = value

            vertical(values, emit)
        return carry

    lax.fori_loop(0, tiles // 8, own_vertical, 0)
    own_halo = halo(own_edge, own_edge_in, 1)
    for copy in own_halo:
        copy.start()

    halo_both(own_edge, own_edge_in, 1).wait_recv()
    for f in range(nf):
        for low, way, keep in edges:
            for e in range(2):
                acc[f, low + e] = acc[f, low + e] + keep * own_edge_in[way, f, e]

    names_all = pltpu.make_async_remote_copy(
        src_ref=label, dst_ref=label_in, send_sem=name_sem.at[0], recv_sem=name_sem.at[1],
        device_id={"horiz": pole}, device_id_type=MESH,
    )
    names_all.wait_recv()
    slot_lane = lax.broadcasted_iota(jnp.int32, (1, tiles), 1)
    arrived = jnp.where(slot_lane < CAP, label_in[0, 0:1], jnp.where(slot_lane < 2 * CAP, label_in[1, 0:1], label_in[2, 0:1]))
    arrived = jnp.where(slot_lane < SLOTS, arrived, -1)
    hit = jnp.where(jnp.broadcast_to(arrived, square) == row, 1.0, 0.0).astype(BF16)[:, :SLOTS]

    whole_piece = (slice(None), pl.ds(2, nl - 4))
    pltpu.make_async_remote_copy(
        src_ref=snd.at[whole_piece], dst_ref=rcv.at[whole_piece], send_sem=z_send, recv_sem=z_recv.at[0],
        device_id={"horiz": pole}, device_id_type=MESH,
    ).wait_recv()

    def finish(m, carry):
        for f in range(nf):
            acc[f, m] = acc[f, m] + spread(hit, rcv[f, m])
        return carry

    lax.fori_loop(2, nl - 2, finish, 0)

    disp_all(part_x, 3, "fld").wait()
    names_all.wait_send()
    halo_both(slot_edge, slot_edge_in, 0).wait_send()
    halo_both(own_edge, own_edge_in, 1).wait_send()
    for f in range(nf):
        for low, _, _ in edges:
            piece = (f, pl.ds(low, 2))
            pltpu.make_async_remote_copy(
                src_ref=snd.at[piece], dst_ref=rcv.at[piece], send_sem=z_send,
                recv_sem=z_recv.at[1 + f * 2 + (0 if low == 0 else 1)],
                device_id={"horiz": pole}, device_id_type=MESH,
            ).wait_recv()
            for e in range(2):
                acc[f, low + e] = acc[f, low + e] + spread(hit, rcv[f, low + e])
    pltpu.make_async_remote_copy(
        src_ref=snd, dst_ref=rcv, send_sem=z_send, recv_sem=z_recv.at[0],
        device_id={"horiz": pole}, device_id_type=MESH,
    ).wait_send()


def deliver(field_ref, disp_ref, field_out, disp_out, sem):
    copies = [
        pltpu.make_async_copy(field_ref, field_out, sem.at[0]),
        pltpu.make_async_copy(disp_ref, disp_out, sem.at[1]),
    ]
    for copy in copies:
        copy.start()
    for copy in copies:
        copy.wait()


def shards(mesh, adj_out, interp, vert_wts, vert_base, dep_tile, traj_grad):
    nf, nl, tiles, cols = adj_out.shape
    blocks, levs, flds = mesh.shape["horiz"], mesh.shape["lev"], mesh.shape["fld"]
    fl = nf * nl
    span = tiles // flds
    short = span // levs
    hbm = pl.BlockSpec(memory_space=pl.ANY)
    vmem = pl.BlockSpec(memory_space=pltpu.VMEM)
    dma = pltpu.SemaphoreType.DMA
    halo_slots = pltpu.VMEM((2, nf, 2, SLOTS, cols), F32)
    halo_own = pltpu.VMEM((2, nf, 2, tiles, cols), F32)
    field, disp = pl.pallas_call(
        functools.partial(kernel, blocks, levs, flds, nf, nl, tiles),
        out_shape=(
            pltpu.VMEM((nf, nl, tiles, cols), F32),
            pltpu.VMEM((2, tiles, cols), F32),
        ),
        in_specs=[hbm] * 6,
        out_specs=(vmem, vmem),
        scratch_shapes=[
            pltpu.VMEM((fl, tiles, cols), BF16),
            pltpu.VMEM((tiles, cols, cols), BF16),
            pltpu.VMEM((2, fl, tiles, cols), BF16),
            pltpu.VMEM((fl * tiles, cols), F32),
            pltpu.VMEM((fl * SLOTS, cols), F32),
            pltpu.VMEM((fl * tiles, cols), F32),
            pltpu.VMEM((nf, nl, SLOTS, cols), F32),
            pltpu.VMEM((nf, nl, SLOTS, cols), F32),
            halo_slots, halo_slots, halo_own, halo_own,
            pltpu.VMEM((1, tiles), jnp.int32),
            pltpu.SMEM((4, nl), F32),
            pltpu.SMEM((nl,), jnp.int32),
            pltpu.VMEM((ROLES, 8, tiles), jnp.int32),
            pltpu.VMEM((ROLES, 8, tiles), jnp.int32),
            pltpu.VMEM((8, tiles), jnp.int32),
            pltpu.SMEM((8, tiles), jnp.int32),
            pltpu.VMEM((2, tiles, cols), F32),
            pltpu.VMEM((flds - 1, 2, span, cols), F32),
            pltpu.VMEM((levs - 1, 2, short, cols), F32),
            pltpu.VMEM((2, tiles, cols), F32),
            dma((6,)), dma, pltpu.SemaphoreType.REGULAR, dma((2,)), dma, dma((1 + 2 * nf,)),
            dma((2,)), dma((2,)), dma((4,)), dma((4,)),
        ],
        compiler_params=pltpu.CompilerParams(
            collective_id=0, has_side_effects=True, vmem_limit_bytes=VMEM_BYTES
        ),
    )(*[
        pltpu.with_memory_space_constraint(x, pltpu.HBM)
        for x in (
            adj_out.reshape(fl, tiles, cols), interp, traj_grad.reshape(2, fl, tiles, cols),
            dep_tile.reshape(1, tiles), vert_wts.T, vert_base,
        )
    ])
    return pl.pallas_call(
        deliver,
        out_shape=(pltpu.HBM(field.shape, F32), pltpu.HBM(disp.shape, F32)),
        in_specs=[vmem] * 2,
        out_specs=(hbm, hbm),
        scratch_shapes=[dma((2,))],
    )(*[pltpu.with_memory_space_constraint(x, pltpu.VMEM) for x in (field, disp)])


def solution(mesh):
    return jax.shard_map(
        functools.partial(shards, mesh),
        mesh=mesh,
        in_specs=(
            P("fld", "lev", "horiz", None),
            P("horiz", None, None),
            P("lev", None),
            P("lev"),
            P("horiz"),
            P(None, "fld", "lev", "horiz", None),
        ),
        out_specs=(P("fld", "lev", "horiz", None), P(None, "horiz", None)),
        check_vma=False,
    )
```

```python
import functools

import jax
import jax.numpy as jnp
from jax import lax
from jax.experimental import pallas as pl
from jax.experimental.pallas import tpu as pltpu
from jax.sharding import PartitionSpec as P

MESH = pl.DeviceIdType.MESH
CAP = 32
ROLES = 3
GROUP = 8
GROUPS = CAP // GROUP
SLOTS = ROLES * CAP
VMEM_BYTES = 48 * 1024 * 1024
KEPT_LOW, KEPT_TOP = 4, 2
F32, BF16 = jnp.float32, jnp.bfloat16


def split(values):
    high = values.astype(BF16)
    low = (values - high.astype(F32)).astype(BF16)
    return jnp.concatenate([high, low], axis=1)


def spread(hit, values):
    both = jnp.dot(hit, split(values), preferred_element_type=F32)
    width = values.shape[1]
    return both[:, :width] + both[:, width:]


def kernel(
    blocks, levs, flds, nf, nl, tiles,
    adj_hbm, interp_hbm, traj_hbm, dep_hbm, wts_hbm, base_hbm,
    acc, disp_ref,
    adj, interp, traj, adj32, h_slot, h_own, snd, rcv,
    slot_edge, slot_edge_in, own_edge, own_edge_in,
    dep_ref, wts_ref, base_ref, label, label_in, index_v, index_s, part, part_x, part_y, whole,
    in_sem, index_sem, answered, name_sem, z_send, z_recv, halo_send, halo_recv, disp_send, disp_recv,
):
    fl = nf * nl
    here, lev, fld = lax.axis_index("horiz"), lax.axis_index("lev"), lax.axis_index("fld")
    core = lax.rem(here, 2)
    pole = lax.rem(here + blocks // 2, blocks)
    across = lax.rem(here + 2 * core - 1 + blocks, blocks)
    mate = here + 1 - 2 * core
    next_x = lax.rem(fld + 1, flds)
    up, down = lax.rem(lev + 1, levs), lax.rem(lev + levs - 1, levs)

    pairs = [
        (dep_hbm, dep_ref), (wts_hbm, wts_ref), (base_hbm, base_ref),
        (adj_hbm, adj), (interp_hbm, interp), (traj_hbm, traj),
    ]
    loads = [pltpu.make_async_copy(src, dst, in_sem.at[i]) for i, (src, dst) in enumerate(pairs)]
    for load in loads[:5]:
        load.start()

    barrier = pltpu.get_barrier_semaphore()
    partners = [pole, across, mate]
    for partner in partners:
        pl.semaphore_signal(barrier, inc=1, device_id={"horiz": partner}, device_id_type=MESH)
    for axis, me, size in (("lev", lev, levs), ("fld", fld, flds)):
        for d in range(1, size):

            @pl.when(me + d < size)
            def _(axis=axis, me=me, d=d):
                pl.semaphore_signal(barrier, inc=1, device_id={axis: me + d}, device_id_type=MESH)

    loads[0].wait()
    square = (tiles, tiles)
    by_lane = jnp.broadcast_to(dep_ref[...], square)
    by_row = by_lane.T
    lane = lax.broadcasted_iota(jnp.int32, square, 1)
    row = lax.broadcasted_iota(jnp.int32, square, 0)

    def role_of(dep):
        owner = dep // tiles
        return jnp.where(owner == pole, 0, jnp.where(owner == across, 1, jnp.where(owner == mate, 2, ROLES)))

    lane_role, row_role = role_of(by_lane), role_of(by_row)
    before = jnp.where((lane_role == row_role) & (row < lane), 1, 0)
    rank = jnp.sum(before, axis=0, keepdims=True)
    slot = jnp.where(lane_role < ROLES, lane_role * CAP + rank, -1)
    chosen = slot.T == lane
    source = jnp.sum(jnp.where(chosen, row, 0), axis=0, keepdims=True)
    target = jnp.sum(jnp.where(chosen, lax.rem(by_row, tiles) + 1, 0), axis=0, keepdims=True) - 1
    index_v[...] = jnp.broadcast_to(source, index_v.shape)
    for r in range(ROLES):
        label[r] = jnp.broadcast_to(target, label.shape[1:])
    index_copy = pltpu.make_async_copy(index_v, index_s, index_sem)
    index_copy.start()
    own_hit = jnp.where((lane_role == ROLES) & (lax.rem(by_lane, tiles) == row), 1.0, 0.0).astype(BF16)

    first = lev * nl
    loads[1].wait()
    loads[2].wait()
    coef = []
    for l in range(nl):
        late = base_ref[l] < first + l
        taps = [wts_ref[j, l] for j in range(4)]
        coef.append([
            jnp.where(late, taps[k] if k < 4 else 0.0, taps[k - 1] if k > 0 else 0.0) for k in range(5)
        ])

    def vertical(values, emit):
        for e in range(nl + 4):
            total = None
            for l in range(max(0, e - 4), min(nl - 1, e) + 1):
                term = coef[l][e - l] * values[l]
                total = term if total is None else total + term
            emit(e, total)

    loads[3].wait()

    def widen(i, carry):
        adj32[pl.ds(pl.multiple_of(i * tiles, tiles), tiles), :] = adj[i].astype(F32)
        return carry

    lax.fori_loop(0, fl, widen, 0)
    index_copy.wait()
    loads[4].wait()
    loads[5].start()

    def horizontal(t, s, dest, extent):
        rows = [adj32[pl.ds(t + b * 8 * tiles, 8, stride=tiles), :] for b in range(fl // 8)]
        value = jnp.dot(jnp.concatenate(rows, axis=0).astype(BF16), interp[t], preferred_element_type=F32)
        for b in range(fl // 8):
            dest[pl.ds(s + b * 8 * extent, 8, stride=extent), :] = value[b * 8 : b * 8 + 8]

    def work(g):
        at = pl.multiple_of(g * GROUP, GROUP)
        for i in range(GROUP):
            horizontal(index_s[0, at + i], at + i, h_slot, SLOTS)
        for f in range(nf):
            values = [
                h_slot[pl.ds(pl.multiple_of((f * nl + l) * SLOTS + at, GROUP), GROUP), :] for l in range(nl)
            ]

            def emit(e, value, f=f):
                if e < 2:
                    slot_edge[0, f, e, pl.ds(at, GROUP), :] = value
                elif e < nl + 2:
                    snd[f, e - 2, pl.ds(at, GROUP), :] = value
                else:
                    slot_edge[1, f, e - nl - 2, pl.ds(at, GROUP), :] = value

            vertical(values, emit)

    def inner(g):
        role = g // GROUPS
        partner = jnp.where(role == 0, pole, jnp.where(role == 1, across, mate))
        at = pl.multiple_of(g * GROUP, GROUP)
        piece = (slice(None), pl.ds(2, nl - 4), pl.ds(at, GROUP), slice(None))
        return pltpu.make_async_remote_copy(
            src_ref=snd.at[piece], dst_ref=rcv.at[piece],
            send_sem=z_send, recv_sem=z_recv.at[jnp.where(role == 0, 0, 1)],
            device_id={"horiz": partner}, device_id_type=MESH,
        )

    work(0)
    pl.semaphore_wait(barrier, ROLES + lev + fld)
    inner(0).start()
    for axis, me, size in (("lev", lev, levs), ("fld", fld, flds)):
        for d in range(1, size):

            @pl.when(me >= d)
            def _(axis=axis, me=me, d=d):
                pl.semaphore_signal(answered, inc=1, device_id={axis: me - d}, device_id_type=MESH)


    def step(g, carry):
        work(g)
        inner(g).start()
        return carry

    def both(g, carry):
        step(GROUPS + g - 1, 0)
        step(g, 0)
        return carry

    lax.fori_loop(1, GROUPS, both, 0)

    loads[5].wait()

    def displacement(b, carry):
        at = pl.multiple_of(b * 16, 16)
        for c in range(2):
            total = None
            for i in range(fl):
                term = adj32[pl.ds(pl.multiple_of(i * tiles + at, 16), 16), :] * traj[c, i, pl.ds(at, 16), :].astype(F32)
                total = term if total is None else total + term
            part[c, pl.ds(at, 16), :] = total
        return carry

    lax.fori_loop(0, tiles // 16, displacement, 0)
    span = tiles // flds
    short = span // levs

    def disp_copy(src, dst, n, axis, target):
        return pltpu.make_async_remote_copy(
            src_ref=src, dst_ref=dst, send_sem=disp_send.at[n], recv_sem=disp_recv.at[n],
            device_id={axis: target}, device_id_type=MESH,
        )

    def disp_all(like, n, axis):
        return disp_copy(like, like, n, axis, next_x if axis == "fld" else up)

    to_x = []
    for d in range(1, flds):
        there = lax.rem(fld + d, flds)
        src = part.at[:, pl.ds(pl.multiple_of(there * span, span), span), :]
        to_x.append(disp_copy(src, part_x.at[d - 1], 0, "fld", there))
    answers = levs - 1 - lev + flds - 1 - fld

    @pl.when(answers > 0)
    def _():
        pl.semaphore_wait(answered, answers)

    for copy in to_x:
        copy.start()

    lax.fori_loop(2 * GROUPS - 1, ROLES * GROUPS, step, 0)

    names = [
        pltpu.make_async_remote_copy(
            src_ref=label.at[r], dst_ref=label_in.at[r], send_sem=name_sem.at[0], recv_sem=name_sem.at[1],
            device_id={"horiz": partners[r]}, device_id_type=MESH,
        )
        for r in range(ROLES)
    ]
    for copy in names:
        copy.start()

    def halo(src, dst, n):
        return [
            pltpu.make_async_remote_copy(
                src_ref=src.at[way], dst_ref=dst.at[way], send_sem=halo_send.at[n], recv_sem=halo_recv.at[n],
                device_id={"lev": target}, device_id_type=MESH,
            )
            for way, target in enumerate((down, up))
        ]

    def halo_both(src, dst, n):
        return pltpu.make_async_remote_copy(
            src_ref=src, dst_ref=dst, send_sem=halo_send.at[n], recv_sem=halo_recv.at[n],
            device_id={"lev": up}, device_id_type=MESH,
        )

    slot_halo = halo(slot_edge, slot_edge_in, 0)
    for copy in slot_halo:
        copy.start()

    disp_all(part_x, 0, "fld").wait_recv()
    mine = pl.multiple_of(fld * span, span)
    total = part[:, pl.ds(mine, span), :]
    for d in range(flds - 1):
        total = total + part_x[d]
    whole[:, pl.ds(mine, span), :] = total
    to_y = []
    for d in range(1, levs):
        there = lax.rem(lev + d, levs)
        src = whole.at[:, pl.ds(pl.multiple_of(mine + there * short, short), short), :]
        to_y.append(disp_copy(src, part_y.at[d - 1], 1, "lev", there))
    for copy in to_y:
        copy.start()

    def own(t, carry):
        horizontal(t, t, h_own, tiles)
        return carry

    lax.fori_loop(0, tiles // 2, own, 0, unroll=8)

    disp_all(part_y, 1, "lev").wait()
    piece = pl.multiple_of(mine + lev * short, short)
    total = whole[:, pl.ds(piece, short), :]
    for d in range(levs - 1):
        total = total + part_y[d]
    part[:, pl.ds(piece, short), :] = total
    back_y = []
    disp_all(part_x, 0, "fld").wait_send()
    for d in range(1, levs):
        there = lax.rem(lev + d, levs)
        at = (slice(None), pl.ds(piece, short), slice(None))
        back_y.append(disp_copy(part.at[at], disp_ref.at[at], 2, "lev", there))
    for copy in back_y:
        copy.start()
    disp_ref[:, pl.ds(piece, short), :] = total

    lax.fori_loop(tiles // 2, tiles, own, 0, unroll=8)

    disp_all(part_y, 2, "lev").wait()
    back_x = []
    for d in range(1, flds):
        there = lax.rem(fld + d, flds)
        at = (slice(None), pl.ds(mine, span), slice(None))
        back_x.append(disp_copy(disp_ref.at[at], disp_ref.at[at], 3, "fld", there))
    for copy in back_x:
        copy.start()


    from_below = jnp.where(lev > 0, 1.0, 0.0).astype(F32)
    from_above = jnp.where(lev < levs - 1, 1.0, 0.0).astype(F32)
    halo_both(slot_edge, slot_edge_in, 0).wait_recv()

    edges = ((0, 1, from_below), (nl - 2, 0, from_above))

    def outer(f, low, r):
        n = 2 + f * 2 + (0 if low == 0 else 1)
        piece = (f, pl.ds(low, 2), pl.ds(r * CAP, CAP), slice(None))
        return pltpu.make_async_remote_copy(
            src_ref=snd.at[piece], dst_ref=rcv.at[piece],
            send_sem=z_send, recv_sem=z_recv.at[n],
            device_id={"horiz": partners[r]}, device_id_type=MESH,
        )

    for f in range(nf):
        for low, way, keep in edges:
            for e in range(2):
                snd[f, low + e] = snd[f, low + e] + keep * slot_edge_in[way, f, e]
            for r in range(1, ROLES):
                outer(f, low, r).start()

    half = blocks // 4
    place = here // 2
    kept = jnp.where(lax.rem(place, half) < half // 2, 0, jnp.where(place < half, KEPT_LOW, KEPT_TOP))
    pieces = [(f, low) for f in range(nf) for low, _, _ in edges]
    for n, (f, low) in enumerate(pieces):

        @pl.when(n < len(pieces) - kept)
        def _(f=f, low=low):
            outer(f, low, 0).start()


    def gather_own(i, carry):
        at = pl.ds(pl.multiple_of(i * tiles, tiles), tiles)
        h_own[at, :] = spread(own_hit, h_own[at, :])
        return carry

    lax.fori_loop(0, fl, gather_own, 0, unroll=2)

    def own_vertical(b, carry):
        at = pl.multiple_of(b * 8, 8)
        for f in range(nf):
            values = [h_own[pl.ds(pl.multiple_of((f * nl + l) * tiles + at, 8), 8), :] for l in range(nl)]

            def emit(e, value, f=f):
                if e < 2:
                    own_edge[0, f, e, pl.ds(at, 8), :] = value
                elif e < nl + 2:
                    acc[f, e - 2, pl.ds(at, 8), :] = value
                else:
                    own_edge[1, f, e - nl - 2, pl.ds(at, 8), :] = value

            vertical(values, emit)
        return carry

    lax.fori_loop(0, tiles // 8, own_vertical, 0)
    own_halo = halo(own_edge, own_edge_in, 1)
    for copy in own_halo:
        copy.start()

    def inner_all(role, roles):
        piece = (slice(None), pl.ds(2, nl - 4), pl.ds(role * CAP, roles * CAP))
        return pltpu.make_async_remote_copy(
            src_ref=snd.at[piece], dst_ref=rcv.at[piece], send_sem=z_send, recv_sem=z_recv.at[role],
            device_id={"horiz": pole}, device_id_type=MESH,
        )

    inner_all(0, 1).wait_recv()
    for n, (f, low) in enumerate(pieces):

        @pl.when(n >= len(pieces) - kept)
        def _(f=f, low=low):
            outer(f, low, 0).start()

    halo_both(own_edge, own_edge_in, 1).wait_recv()
    for f in range(nf):
        for low, way, keep in edges:
            for e in range(2):
                acc[f, low + e] = acc[f, low + e] + keep * own_edge_in[way, f, e]

    names_all = pltpu.make_async_remote_copy(
        src_ref=label, dst_ref=label_in, send_sem=name_sem.at[0], recv_sem=name_sem.at[1],
        device_id={"horiz": pole}, device_id_type=MESH,
    )
    names_all.wait_recv()
    slot_lane = lax.broadcasted_iota(jnp.int32, (1, tiles), 1)
    arrived = jnp.where(slot_lane < CAP, label_in[0, 0:1], jnp.where(slot_lane < 2 * CAP, label_in[1, 0:1], label_in[2, 0:1]))
    arrived = jnp.where(slot_lane < SLOTS, arrived, -1)
    hit = jnp.where(jnp.broadcast_to(arrived, square) == row, 1.0, 0.0).astype(BF16)[:, :SLOTS]

    inner_all(1, ROLES - 1).wait_recv()

    def finish(m, carry):
        for f in range(nf):
            acc[f, m] = acc[f, m] + spread(hit, rcv[f, m])
        return carry

    lax.fori_loop(2, nl - 2, finish, 0)

    disp_all(part_x, 3, "fld").wait()
    names_all.wait_send()
    halo_both(slot_edge, slot_edge_in, 0).wait_send()
    halo_both(own_edge, own_edge_in, 1).wait_send()
    for f in range(nf):
        for low, _, _ in edges:
            piece = (f, pl.ds(low, 2))
            pltpu.make_async_remote_copy(
                src_ref=snd.at[piece], dst_ref=rcv.at[piece], send_sem=z_send,
                recv_sem=z_recv.at[2 + f * 2 + (0 if low == 0 else 1)],
                device_id={"horiz": pole}, device_id_type=MESH,
            ).wait_recv()
            for e in range(2):
                acc[f, low + e] = acc[f, low + e] + spread(hit, rcv[f, low + e])
    pltpu.make_async_remote_copy(
        src_ref=snd, dst_ref=rcv, send_sem=z_send, recv_sem=z_recv.at[0],
        device_id={"horiz": pole}, device_id_type=MESH,
    ).wait_send()


def deliver(field_ref, disp_ref, field_out, disp_out, sem):
    copies = [
        pltpu.make_async_copy(field_ref, field_out, sem.at[0]),
        pltpu.make_async_copy(disp_ref, disp_out, sem.at[1]),
    ]
    for copy in copies:
        copy.start()
    for copy in copies:
        copy.wait()


def shards(mesh, adj_out, interp, vert_wts, vert_base, dep_tile, traj_grad):
    nf, nl, tiles, cols = adj_out.shape
    blocks, levs, flds = mesh.shape["horiz"], mesh.shape["lev"], mesh.shape["fld"]
    fl = nf * nl
    span = tiles // flds
    short = span // levs
    hbm = pl.BlockSpec(memory_space=pl.ANY)
    vmem = pl.BlockSpec(memory_space=pltpu.VMEM)
    dma = pltpu.SemaphoreType.DMA
    halo_slots = pltpu.VMEM((2, nf, 2, SLOTS, cols), F32)
    halo_own = pltpu.VMEM((2, nf, 2, tiles, cols), F32)
    field, disp = pl.pallas_call(
        functools.partial(kernel, blocks, levs, flds, nf, nl, tiles),
        out_shape=(
            pltpu.VMEM((nf, nl, tiles, cols), F32),
            pltpu.VMEM((2, tiles, cols), F32),
        ),
        in_specs=[hbm] * 6,
        out_specs=(vmem, vmem),
        scratch_shapes=[
            pltpu.VMEM((fl, tiles, cols), BF16),
            pltpu.VMEM((tiles, cols, cols), BF16),
            pltpu.VMEM((2, fl, tiles, cols), BF16),
            pltpu.VMEM((fl * tiles, cols), F32),
            pltpu.VMEM((fl * SLOTS, cols), F32),
            pltpu.VMEM((fl * tiles, cols), F32),
            pltpu.VMEM((nf, nl, SLOTS, cols), F32),
            pltpu.VMEM((nf, nl, SLOTS, cols), F32),
            halo_slots, halo_slots, halo_own, halo_own,
            pltpu.VMEM((1, tiles), jnp.int32),
            pltpu.SMEM((4, nl), F32),
            pltpu.SMEM((nl,), jnp.int32),
            pltpu.VMEM((ROLES, 8, tiles), jnp.int32),
            pltpu.VMEM((ROLES, 8, tiles), jnp.int32),
            pltpu.VMEM((8, tiles), jnp.int32),
            pltpu.SMEM((8, tiles), jnp.int32),
            pltpu.VMEM((2, tiles, cols), F32),
            pltpu.VMEM((flds - 1, 2, span, cols), F32),
            pltpu.VMEM((levs - 1, 2, short, cols), F32),
            pltpu.VMEM((2, tiles, cols), F32),
            dma((6,)), dma, pltpu.SemaphoreType.REGULAR, dma((2,)), dma, dma((2 + 2 * nf,)),
            dma((2,)), dma((2,)), dma((4,)), dma((4,)),
        ],
        compiler_params=pltpu.CompilerParams(
            collective_id=0, has_side_effects=True, vmem_limit_bytes=VMEM_BYTES
        ),
    )(*[
        pltpu.with_memory_space_constraint(x, pltpu.HBM)
        for x in (
            adj_out.reshape(fl, tiles, cols), interp, traj_grad.reshape(2, fl, tiles, cols),
            dep_tile.reshape(1, tiles), vert_wts.T, vert_base,
        )
    ])
    return pl.pallas_call(
        deliver,
        out_shape=(pltpu.HBM(field.shape, F32), pltpu.HBM(disp.shape, F32)),
        in_specs=[vmem] * 2,
        out_specs=(hbm, hbm),
        scratch_shapes=[dma((2,))],
    )(*[pltpu.with_memory_space_constraint(x, pltpu.VMEM) for x in (field, disp)])


def solution(mesh):
    return jax.shard_map(
        functools.partial(shards, mesh),
        mesh=mesh,
        in_specs=(
            P("fld", "lev", "horiz", None),
            P("horiz", None, None),
            P("lev", None),
            P("lev"),
            P("horiz"),
            P(None, "fld", "lev", "horiz", None),
        ),
        out_specs=(P("fld", "lev", "horiz", None), P(None, "horiz", None)),
        check_vma=False,
    )
```

```python
import functools

import jax
import jax.numpy as jnp
from jax import lax
from jax.experimental import pallas as pl
from jax.experimental.pallas import tpu as pltpu
from jax.sharding import PartitionSpec as P

MESH = pl.DeviceIdType.MESH
CAP = 32
ROLES = 3
GROUP = 8
GROUPS = CAP // GROUP
SLOTS = ROLES * CAP
VMEM_BYTES = 48 * 1024 * 1024
KEPT_LOW, KEPT_TOP = 4, 2
F32, BF16 = jnp.float32, jnp.bfloat16


def split(values):
    high = values.astype(BF16)
    low = (values - high.astype(F32)).astype(BF16)
    return jnp.concatenate([high, low], axis=1)


def spread(hit, values):
    both = jnp.dot(hit, split(values), preferred_element_type=F32)
    width = values.shape[1]
    return both[:, :width] + both[:, width:]


def kernel(
    blocks, levs, flds, nf, nl, tiles,
    adj_hbm, interp_hbm, traj_hbm, dep_hbm, wts_hbm, base_hbm,
    acc, disp_ref,
    adj, interp, traj, adj32, h_slot, h_own, snd, rcv,
    slot_edge, slot_edge_in, own_edge, own_edge_in,
    dep_ref, wts_ref, base_ref, label, label_in, index_v, index_s, part, part_x, part_y, whole,
    in_sem, answered, name_sem, z_send, z_recv, halo_send, halo_recv, disp_send, disp_recv,
):
    fl = nf * nl
    here, lev, fld = lax.axis_index("horiz"), lax.axis_index("lev"), lax.axis_index("fld")
    core = lax.rem(here, 2)
    pole = lax.rem(here + blocks // 2, blocks)
    across = lax.rem(here + 2 * core - 1 + blocks, blocks)
    mate = here + 1 - 2 * core
    next_x = lax.rem(fld + 1, flds)
    up, down = lax.rem(lev + 1, levs), lax.rem(lev + levs - 1, levs)

    pairs = [
        (dep_hbm, dep_ref), (wts_hbm, wts_ref), (base_hbm, base_ref),
        (adj_hbm, adj), (interp_hbm, interp), (traj_hbm, traj),
    ]
    loads = [pltpu.make_async_copy(src, dst, in_sem.at[i % 5]) for i, (src, dst) in enumerate(pairs)]
    for load in loads[:5]:
        load.start()

    barrier = pltpu.get_barrier_semaphore()
    partners = [pole, across, mate]
    for partner in partners:
        pl.semaphore_signal(barrier, inc=1, device_id={"horiz": partner}, device_id_type=MESH)
    for axis, me, size in (("lev", lev, levs), ("fld", fld, flds)):
        for d in range(1, size):

            @pl.when(me + d < size)
            def _(axis=axis, me=me, d=d):
                pl.semaphore_signal(barrier, inc=1, device_id={axis: me + d}, device_id_type=MESH)

    loads[0].wait()
    square = (tiles, tiles)
    by_lane = jnp.broadcast_to(dep_ref[...], square)
    by_row = by_lane.T
    lane = lax.broadcasted_iota(jnp.int32, square, 1)
    row = lax.broadcasted_iota(jnp.int32, square, 0)

    def role_of(dep):
        owner = dep // tiles
        return jnp.where(owner == pole, 0, jnp.where(owner == across, 1, jnp.where(owner == mate, 2, ROLES)))

    lane_role, row_role = role_of(by_lane), role_of(by_row)
    before = jnp.where((lane_role == row_role) & (row < lane), 1, 0)
    rank = jnp.sum(before, axis=0, keepdims=True)
    slot = jnp.where(lane_role < ROLES, lane_role * CAP + rank, -1)
    chosen = slot.T == lane
    source = jnp.sum(jnp.where(chosen, row, 0), axis=0, keepdims=True)
    target = jnp.sum(jnp.where(chosen, lax.rem(by_row, tiles) + 1, 0), axis=0, keepdims=True) - 1
    index_v[...] = jnp.broadcast_to(source, index_v.shape)
    for r in range(ROLES):
        label[r] = jnp.broadcast_to(target, label.shape[1:])
    index_copy = pltpu.make_async_copy(index_v, index_s, in_sem.at[0])
    index_copy.start()
    own_hit = jnp.where((lane_role == ROLES) & (lax.rem(by_lane, tiles) == row), 1.0, 0.0).astype(BF16)

    first = lev * nl
    loads[1].wait()
    loads[2].wait()
    coef = []
    for l in range(nl):
        late = base_ref[l] < first + l
        taps = [wts_ref[j, l] for j in range(4)]
        coef.append([
            jnp.where(late, taps[k] if k < 4 else 0.0, taps[k - 1] if k > 0 else 0.0) for k in range(5)
        ])

    def vertical(values, emit):
        for e in range(nl + 4):
            total = None
            for l in range(max(0, e - 4), min(nl - 1, e) + 1):
                term = coef[l][e - l] * values[l]
                total = term if total is None else total + term
            emit(e, total)

    loads[3].wait()

    def widen(i, carry):
        adj32[pl.ds(pl.multiple_of(i * tiles, tiles), tiles), :] = adj[i].astype(F32)
        return carry

    lax.fori_loop(0, fl, widen, 0)
    index_copy.wait()
    loads[4].wait()
    loads[5].start()

    def horizontal(t, s, dest, extent):
        rows = [adj32[pl.ds(t + b * 8 * tiles, 8, stride=tiles), :] for b in range(fl // 8)]
        value = jnp.dot(jnp.concatenate(rows, axis=0).astype(BF16), interp[t], preferred_element_type=F32)
        for b in range(fl // 8):
            dest[pl.ds(s + b * 8 * extent, 8, stride=extent), :] = value[b * 8 : b * 8 + 8]

    def work(g):
        at = pl.multiple_of(g * GROUP, GROUP)
        for i in range(GROUP):
            horizontal(index_s[0, at + i], at + i, h_slot, SLOTS)
        for f in range(nf):
            values = [
                h_slot[pl.ds(pl.multiple_of((f * nl + l) * SLOTS + at, GROUP), GROUP), :] for l in range(nl)
            ]

            def emit(e, value, f=f):
                if e < 2:
                    slot_edge[0, f, e, pl.ds(at, GROUP), :] = value
                elif e < nl + 2:
                    snd[f, e - 2, pl.ds(at, GROUP), :] = value
                else:
                    slot_edge[1, f, e - nl - 2, pl.ds(at, GROUP), :] = value

            vertical(values, emit)

    def inner(g):
        role = g // GROUPS
        partner = jnp.where(role == 0, pole, jnp.where(role == 1, across, mate))
        at = pl.multiple_of(g * GROUP, GROUP)
        piece = (slice(None), pl.ds(2, nl - 4), pl.ds(at, GROUP), slice(None))
        return pltpu.make_async_remote_copy(
            src_ref=snd.at[piece], dst_ref=rcv.at[piece],
            send_sem=z_send, recv_sem=z_recv.at[jnp.where(role == 0, 0, 1)],
            device_id={"horiz": partner}, device_id_type=MESH,
        )

    work(0)
    pl.semaphore_wait(barrier, ROLES + lev + fld)
    inner(0).start()
    for axis, me, size in (("lev", lev, levs), ("fld", fld, flds)):
        for d in range(1, size):

            @pl.when(me >= d)
            def _(axis=axis, me=me, d=d):
                pl.semaphore_signal(answered, inc=1, device_id={axis: me - d}, device_id_type=MESH)


    def step(g, carry):
        work(g)
        inner(g).start()
        return carry

    def both(g, carry):
        step(GROUPS + g - 1, 0)
        step(g, 0)
        return carry

    lax.fori_loop(1, GROUPS, both, 0)

    loads[5].wait()

    def displacement(b, carry):
        at = pl.multiple_of(b * 16, 16)
        for c in range(2):
            total = None
            for i in range(fl):
                term = adj32[pl.ds(pl.multiple_of(i * tiles + at, 16), 16), :] * traj[c, i, pl.ds(at, 16), :].astype(F32)
                total = term if total is None else total + term
            part[c, pl.ds(at, 16), :] = total
        return carry

    lax.fori_loop(0, tiles // 16, displacement, 0)
    span = tiles // flds
    short = span // levs

    def disp_copy(src, dst, n, axis, target):
        return pltpu.make_async_remote_copy(
            src_ref=src, dst_ref=dst, send_sem=disp_send.at[n], recv_sem=disp_recv.at[n],
            device_id={axis: target}, device_id_type=MESH,
        )

    def disp_all(like, n, axis):
        return disp_copy(like, like, n, axis, next_x if axis == "fld" else up)

    to_x = []
    for d in range(1, flds):
        there = lax.rem(fld + d, flds)
        src = part.at[:, pl.ds(pl.multiple_of(there * span, span), span), :]
        to_x.append(disp_copy(src, part_x.at[d - 1], 0, "fld", there))
    answers = levs - 1 - lev + flds - 1 - fld

    @pl.when(answers > 0)
    def _():
        pl.semaphore_wait(answered, answers)

    for copy in to_x:
        copy.start()

    lax.fori_loop(2 * GROUPS - 1, ROLES * GROUPS, step, 0)

    names = [
        pltpu.make_async_remote_copy(
            src_ref=label.at[r], dst_ref=label_in.at[r], send_sem=name_sem.at[0], recv_sem=name_sem.at[1],
            device_id={"horiz": partners[r]}, device_id_type=MESH,
        )
        for r in range(ROLES)
    ]
    for copy in names:
        copy.start()

    def halo(src, dst, n):
        return [
            pltpu.make_async_remote_copy(
                src_ref=src.at[way], dst_ref=dst.at[way], send_sem=halo_send.at[n], recv_sem=halo_recv.at[n],
                device_id={"lev": target}, device_id_type=MESH,
            )
            for way, target in enumerate((down, up))
        ]

    def halo_both(src, dst, n):
        return pltpu.make_async_remote_copy(
            src_ref=src, dst_ref=dst, send_sem=halo_send.at[n], recv_sem=halo_recv.at[n],
            device_id={"lev": up}, device_id_type=MESH,
        )

    slot_halo = halo(slot_edge, slot_edge_in, 0)
    for copy in slot_halo:
        copy.start()

    disp_all(part_x, 0, "fld").wait_recv()
    mine = pl.multiple_of(fld * span, span)
    total = part[:, pl.ds(mine, span), :]
    for d in range(flds - 1):
        total = total + part_x[d]
    whole[:, pl.ds(mine, span), :] = total
    to_y = []
    for d in range(1, levs):
        there = lax.rem(lev + d, levs)
        src = whole.at[:, pl.ds(pl.multiple_of(mine + there * short, short), short), :]
        to_y.append(disp_copy(src, part_y.at[d - 1], 1, "lev", there))
    for copy in to_y:
        copy.start()

    def own(t, carry):
        horizontal(t, t, h_own, tiles)
        return carry

    lax.fori_loop(0, tiles // 2, own, 0, unroll=8)

    disp_all(part_y, 1, "lev").wait()
    piece = pl.multiple_of(mine + lev * short, short)
    total = whole[:, pl.ds(piece, short), :]
    for d in range(levs - 1):
        total = total + part_y[d]
    part[:, pl.ds(piece, short), :] = total
    back_y = []
    disp_all(part_x, 0, "fld").wait_send()
    for d in range(1, levs):
        there = lax.rem(lev + d, levs)
        at = (slice(None), pl.ds(piece, short), slice(None))
        back_y.append(disp_copy(part.at[at], disp_ref.at[at], 2, "lev", there))
    for copy in back_y:
        copy.start()
    disp_ref[:, pl.ds(piece, short), :] = total

    lax.fori_loop(tiles // 2, tiles, own, 0, unroll=8)

    disp_all(part_y, 2, "lev").wait()
    back_x = []
    for d in range(1, flds):
        there = lax.rem(fld + d, flds)
        at = (slice(None), pl.ds(mine, span), slice(None))
        back_x.append(disp_copy(disp_ref.at[at], disp_ref.at[at], 3, "fld", there))
    for copy in back_x:
        copy.start()


    from_below = jnp.where(lev > 0, 1.0, 0.0).astype(F32)
    from_above = jnp.where(lev < levs - 1, 1.0, 0.0).astype(F32)
    halo_both(slot_edge, slot_edge_in, 0).wait_recv()

    edges = ((0, 1, from_below), (nl - 2, 0, from_above))

    def outer(f, low, r):
        n = 2 + f * 2 + (0 if low == 0 else 1)
        piece = (f, pl.ds(low, 2), pl.ds(r * CAP, CAP), slice(None))
        return pltpu.make_async_remote_copy(
            src_ref=snd.at[piece], dst_ref=rcv.at[piece],
            send_sem=z_send, recv_sem=z_recv.at[n],
            device_id={"horiz": partners[r]}, device_id_type=MESH,
        )

    for f in range(nf):
        for low, way, keep in edges:
            for e in range(2):
                snd[f, low + e] = snd[f, low + e] + keep * slot_edge_in[way, f, e]
            for r in range(1, ROLES):
                outer(f, low, r).start()

    half = blocks // 4
    place = here // 2
    kept = jnp.where(lax.rem(place, half) < half // 2, 0, jnp.where(place < half, KEPT_LOW, KEPT_TOP))
    pieces = [(f, low) for f in range(nf) for low, _, _ in edges]
    for n, (f, low) in enumerate(pieces):

        @pl.when(n < len(pieces) - kept)
        def _(f=f, low=low):
            outer(f, low, 0).start()


    def gather_own(i, carry):
        at = pl.ds(pl.multiple_of(i * tiles, tiles), tiles)
        h_own[at, :] = spread(own_hit, h_own[at, :])
        return carry

    lax.fori_loop(0, fl, gather_own, 0, unroll=2)

    def own_vertical(b, carry):
        at = pl.multiple_of(b * 8, 8)
        for f in range(nf):
            values = [h_own[pl.ds(pl.multiple_of((f * nl + l) * tiles + at, 8), 8), :] for l in range(nl)]

            def emit(e, value, f=f):
                if e < 2:
                    own_edge[0, f, e, pl.ds(at, 8), :] = value
                elif e < nl + 2:
                    acc[f, e - 2, pl.ds(at, 8), :] = value
                else:
                    own_edge[1, f, e - nl - 2, pl.ds(at, 8), :] = value

            vertical(values, emit)
        return carry

    lax.fori_loop(0, tiles // 8, own_vertical, 0)
    own_halo = halo(own_edge, own_edge_in, 1)
    for copy in own_halo:
        copy.start()

    def inner_all(role, roles):
        piece = (slice(None), pl.ds(2, nl - 4), pl.ds(role * CAP, roles * CAP))
        return pltpu.make_async_remote_copy(
            src_ref=snd.at[piece], dst_ref=rcv.at[piece], send_sem=z_send, recv_sem=z_recv.at[role],
            device_id={"horiz": pole}, device_id_type=MESH,
        )

    inner_all(0, 1).wait_recv()
    for n, (f, low) in enumerate(pieces):

        @pl.when(n >= len(pieces) - kept)
        def _(f=f, low=low):
            outer(f, low, 0).start()

    halo_both(own_edge, own_edge_in, 1).wait_recv()
    for f in range(nf):
        for low, way, keep in edges:
            for e in range(2):
                acc[f, low + e] = acc[f, low + e] + keep * own_edge_in[way, f, e]

    names_all = pltpu.make_async_remote_copy(
        src_ref=label, dst_ref=label_in, send_sem=name_sem.at[0], recv_sem=name_sem.at[1],
        device_id={"horiz": pole}, device_id_type=MESH,
    )
    names_all.wait_recv()
    slot_lane = lax.broadcasted_iota(jnp.int32, (1, tiles), 1)
    arrived = jnp.where(slot_lane < CAP, label_in[0, 0:1], jnp.where(slot_lane < 2 * CAP, label_in[1, 0:1], label_in[2, 0:1]))
    arrived = jnp.where(slot_lane < SLOTS, arrived, -1)
    hit = jnp.where(jnp.broadcast_to(arrived, square) == row, 1.0, 0.0).astype(BF16)[:, :SLOTS]

    inner_all(1, ROLES - 1).wait_recv()

    def finish(m, carry):
        for f in range(nf):
            acc[f, m] = acc[f, m] + spread(hit, rcv[f, m])
        return carry

    lax.fori_loop(2, nl - 2, finish, 0)

    disp_all(part_x, 3, "fld").wait()
    names_all.wait_send()
    halo_both(slot_edge, slot_edge_in, 0).wait_send()
    halo_both(own_edge, own_edge_in, 1).wait_send()
    for f in range(nf):
        for low, _, _ in edges:
            piece = (f, pl.ds(low, 2))
            pltpu.make_async_remote_copy(
                src_ref=snd.at[piece], dst_ref=rcv.at[piece], send_sem=z_send,
                recv_sem=z_recv.at[2 + f * 2 + (0 if low == 0 else 1)],
                device_id={"horiz": pole}, device_id_type=MESH,
            ).wait_recv()
            for e in range(2):
                acc[f, low + e] = acc[f, low + e] + spread(hit, rcv[f, low + e])
    pltpu.make_async_remote_copy(
        src_ref=snd, dst_ref=rcv, send_sem=z_send, recv_sem=z_recv.at[0],
        device_id={"horiz": pole}, device_id_type=MESH,
    ).wait_send()


def deliver(field_ref, disp_ref, field_out, disp_out, sem):
    copies = [
        pltpu.make_async_copy(field_ref, field_out, sem.at[0]),
        pltpu.make_async_copy(disp_ref, disp_out, sem.at[1]),
    ]
    for copy in copies:
        copy.start()
    for copy in copies:
        copy.wait()


def shards(mesh, adj_out, interp, vert_wts, vert_base, dep_tile, traj_grad):
    nf, nl, tiles, cols = adj_out.shape
    blocks, levs, flds = mesh.shape["horiz"], mesh.shape["lev"], mesh.shape["fld"]
    fl = nf * nl
    span = tiles // flds
    short = span // levs
    hbm = pl.BlockSpec(memory_space=pl.ANY)
    vmem = pl.BlockSpec(memory_space=pltpu.VMEM)
    dma = pltpu.SemaphoreType.DMA
    halo_slots = pltpu.VMEM((2, nf, 2, SLOTS, cols), F32)
    halo_own = pltpu.VMEM((2, nf, 2, tiles, cols), F32)
    field, disp = pl.pallas_call(
        functools.partial(kernel, blocks, levs, flds, nf, nl, tiles),
        out_shape=(
            pltpu.VMEM((nf, nl, tiles, cols), F32),
            pltpu.VMEM((2, tiles, cols), F32),
        ),
        in_specs=[hbm] * 6,
        out_specs=(vmem, vmem),
        scratch_shapes=[
            pltpu.VMEM((fl, tiles, cols), BF16),
            pltpu.VMEM((tiles, cols, cols), BF16),
            pltpu.VMEM((2, fl, tiles, cols), BF16),
            pltpu.VMEM((fl * tiles + tiles, cols), F32),
            pltpu.VMEM((fl * SLOTS + SLOTS, cols), F32),
            pltpu.VMEM((fl * tiles + tiles, cols), F32),
            pltpu.VMEM((nf, nl, SLOTS, cols), F32),
            pltpu.VMEM((nf, nl, SLOTS, cols), F32),
            halo_slots, halo_slots, halo_own, halo_own,
            pltpu.VMEM((1, tiles), jnp.int32),
            pltpu.SMEM((4, nl), F32),
            pltpu.SMEM((nl,), jnp.int32),
            pltpu.VMEM((ROLES, 8, tiles), jnp.int32),
            pltpu.VMEM((ROLES, 8, tiles), jnp.int32),
            pltpu.VMEM((8, tiles), jnp.int32),
            pltpu.SMEM((8, tiles), jnp.int32),
            pltpu.VMEM((2, tiles, cols), F32),
            pltpu.VMEM((flds - 1, 2, span, cols), F32),
            pltpu.VMEM((levs - 1, 2, short, cols), F32),
            pltpu.VMEM((2, tiles, cols), F32),
            dma((5,)), pltpu.SemaphoreType.REGULAR, dma((2,)), dma, dma((2 + 2 * nf,)),
            dma((2,)), dma((2,)), dma((4,)), dma((4,)),
        ],
        compiler_params=pltpu.CompilerParams(
            collective_id=0, has_side_effects=True, vmem_limit_bytes=VMEM_BYTES
        ),
    )(*[
        pltpu.with_memory_space_constraint(x, pltpu.HBM)
        for x in (
            adj_out.reshape(fl, tiles, cols), interp, traj_grad.reshape(2, fl, tiles, cols),
            dep_tile.reshape(1, tiles), vert_wts.T, vert_base,
        )
    ])
    return pl.pallas_call(
        deliver,
        out_shape=(pltpu.HBM(field.shape, F32), pltpu.HBM(disp.shape, F32)),
        in_specs=[vmem] * 2,
        out_specs=(hbm, hbm),
        scratch_shapes=[dma((2,))],
    )(*[pltpu.with_memory_space_constraint(x, pltpu.VMEM) for x in (field, disp)])


def solution(mesh):
    return jax.shard_map(
        functools.partial(shards, mesh),
        mesh=mesh,
        in_specs=(
            P("fld", "lev", "horiz", None),
            P("horiz", None, None),
            P("lev", None),
            P("lev"),
            P("horiz"),
            P(None, "fld", "lev", "horiz", None),
        ),
        out_specs=(P("fld", "lev", "horiz", None), P(None, "horiz", None)),
        check_vma=False,
    )
```

```python
import functools

import jax
import jax.numpy as jnp
from jax import lax
from jax.experimental import pallas as pl
from jax.experimental.pallas import tpu as pltpu
from jax.sharding import PartitionSpec as P

MESH = pl.DeviceIdType.MESH
CAP = 32
ROLES = 3
GROUP = 8
GROUPS = CAP // GROUP
SLOTS = ROLES * CAP
VMEM_BYTES = 48 * 1024 * 1024
KEPT_LOW, KEPT_TOP = 4, 2
F32, BF16 = jnp.float32, jnp.bfloat16


def split(values):
    high = values.astype(BF16)
    low = (values - high.astype(F32)).astype(BF16)
    return jnp.concatenate([high, low], axis=1)


def spread(hit, values):
    both = jnp.dot(hit, split(values), preferred_element_type=F32)
    width = values.shape[1]
    return both[:, :width] + both[:, width:]


def kernel(
    blocks, levs, flds, nf, nl, tiles,
    adj_hbm, interp_hbm, traj_hbm, dep_hbm, wts_hbm, base_hbm,
    acc, disp_ref,
    adj, interp, traj, adj32, h_slot, h_own, snd, rcv,
    slot_edge, slot_edge_in, own_edge, own_edge_in,
    dep_ref, wts_ref, base_ref, label, label_in, index_v, index_s, part, part_x, part_y, whole,
    in_sem, answered, name_sem, z_send, z_recv, halo_send, halo_recv, disp_send, disp_recv,
):
    fl = nf * nl
    here, lev, fld = lax.axis_index("horiz"), lax.axis_index("lev"), lax.axis_index("fld")
    core = lax.rem(here, 2)
    pole = lax.rem(here + blocks // 2, blocks)
    across = lax.rem(here + 2 * core - 1 + blocks, blocks)
    mate = here + 1 - 2 * core
    next_x = lax.rem(fld + 1, flds)
    up, down = lax.rem(lev + 1, levs), lax.rem(lev + levs - 1, levs)

    pairs = [
        (dep_hbm, dep_ref), (wts_hbm, wts_ref), (base_hbm, base_ref),
        (adj_hbm, adj), (interp_hbm, interp), (traj_hbm, traj),
    ]
    loads = [pltpu.make_async_copy(src, dst, in_sem.at[i % 5]) for i, (src, dst) in enumerate(pairs)]
    for load in loads[:5]:
        load.start()

    barrier = pltpu.get_barrier_semaphore()
    partners = [pole, across, mate]
    for partner in partners:
        pl.semaphore_signal(barrier, inc=1, device_id={"horiz": partner}, device_id_type=MESH)
    for axis, me, size in (("lev", lev, levs), ("fld", fld, flds)):
        for d in range(1, size):

            @pl.when(me + d < size)
            def _(axis=axis, me=me, d=d):
                pl.semaphore_signal(barrier, inc=1, device_id={axis: me + d}, device_id_type=MESH)

    loads[0].wait()
    square = (tiles, tiles)
    by_lane = jnp.broadcast_to(dep_ref[...], square)
    by_row = by_lane.T
    lane = lax.broadcasted_iota(jnp.int32, square, 1)
    row = lax.broadcasted_iota(jnp.int32, square, 0)

    def role_of(dep):
        owner = dep // tiles
        return jnp.where(owner == pole, 0, jnp.where(owner == across, 1, jnp.where(owner == mate, 2, ROLES)))

    lane_role, row_role = role_of(by_lane), role_of(by_row)
    before = jnp.where((lane_role == row_role) & (row < lane), 1, 0)
    rank = jnp.sum(before, axis=0, keepdims=True)
    slot = jnp.where(lane_role < ROLES, lane_role * CAP + rank, -1)
    chosen = slot.T == lane
    source = jnp.sum(jnp.where(chosen, row, 0), axis=0, keepdims=True)
    target = jnp.sum(jnp.where(chosen, lax.rem(by_row, tiles) + 1, 0), axis=0, keepdims=True) - 1
    index_v[...] = jnp.broadcast_to(source, index_v.shape)
    for r in range(ROLES):
        label[r] = jnp.broadcast_to(target, label.shape[1:])
    index_copy = pltpu.make_async_copy(index_v, index_s, in_sem.at[0])
    index_copy.start()
    own_hit = jnp.where((lane_role == ROLES) & (lax.rem(by_lane, tiles) == row), 1.0, 0.0).astype(BF16)

    first = lev * nl
    loads[1].wait()
    loads[2].wait()
    coef = []
    for l in range(nl):
        late = base_ref[l] < first + l
        taps = [wts_ref[j, l] for j in range(4)]
        coef.append([
            jnp.where(late, taps[k] if k < 4 else 0.0, taps[k - 1] if k > 0 else 0.0) for k in range(5)
        ])

    def vertical(values, emit):
        for e in range(nl + 4):
            total = None
            for l in range(max(0, e - 4), min(nl - 1, e) + 1):
                term = coef[l][e - l] * values[l]
                total = term if total is None else total + term
            emit(e, total)

    loads[3].wait()

    def widen(i, carry):
        adj32[pl.ds(pl.multiple_of(i * tiles, tiles), tiles), :] = adj[i].astype(F32)
        return carry

    lax.fori_loop(0, fl, widen, 0)
    index_copy.wait()
    loads[4].wait()
    loads[5].start()

    def horizontal(t, s, dest, extent):
        rows = [adj32[pl.ds(t + b * 8 * tiles, 8, stride=tiles), :] for b in range(fl // 8)]
        value = jnp.dot(jnp.concatenate(rows, axis=0).astype(BF16), interp[t], preferred_element_type=F32)
        for b in range(fl // 8):
            dest[pl.ds(s + b * 8 * extent, 8, stride=extent), :] = value[b * 8 : b * 8 + 8]

    def work(g, send=None):
        at = pl.multiple_of(g * GROUP, GROUP)
        for i in range(GROUP):
            horizontal(index_s[0, at + i], at + i, h_slot, SLOTS)
        for f in range(nf):
            values = [
                h_slot[pl.ds(pl.multiple_of((f * nl + l) * SLOTS + at, GROUP), GROUP), :] for l in range(nl)
            ]

            def emit(e, value, f=f):
                if e < 2:
                    slot_edge[0, f, e, pl.ds(at, GROUP), :] = value
                elif e < nl + 2:
                    snd[f, e - 2, pl.ds(at, GROUP), :] = value
                else:
                    slot_edge[1, f, e - nl - 2, pl.ds(at, GROUP), :] = value

            vertical(values, emit)
            if send is not None:
                send(g, f)

    def inner(g, f):
        role = g // GROUPS
        partner = jnp.where(role == 0, pole, jnp.where(role == 1, across, mate))
        at = pl.multiple_of(g * GROUP, GROUP)
        piece = (f, pl.ds(2, nl - 4), pl.ds(at, GROUP), slice(None))
        return pltpu.make_async_remote_copy(
            src_ref=snd.at[piece], dst_ref=rcv.at[piece],
            send_sem=z_send, recv_sem=z_recv.at[jnp.where(role == 0, 0, 1)],
            device_id={"horiz": partner}, device_id_type=MESH,
        )

    work(0)
    pl.semaphore_wait(barrier, ROLES + lev + fld)
    for f in range(nf):
        inner(0, f).start()
    for axis, me, size in (("lev", lev, levs), ("fld", fld, flds)):
        for d in range(1, size):

            @pl.when(me >= d)
            def _(axis=axis, me=me, d=d):
                pl.semaphore_signal(answered, inc=1, device_id={axis: me - d}, device_id_type=MESH)


    def step(g, carry):
        work(g, lambda g, f: inner(g, f).start())
        return carry

    def both(g, carry):
        step(GROUPS + g - 1, 0)
        step(g, 0)
        return carry

    lax.fori_loop(1, GROUPS, both, 0)

    loads[5].wait()

    def displacement(b, carry):
        at = pl.multiple_of(b * 16, 16)
        for c in range(2):
            total = None
            for i in range(fl):
                term = adj32[pl.ds(pl.multiple_of(i * tiles + at, 16), 16), :] * traj[c, i, pl.ds(at, 16), :].astype(F32)
                total = term if total is None else total + term
            part[c, pl.ds(at, 16), :] = total
        return carry

    lax.fori_loop(0, tiles // 16, displacement, 0)
    span = tiles // flds
    short = span // levs

    def disp_copy(src, dst, n, axis, target):
        return pltpu.make_async_remote_copy(
            src_ref=src, dst_ref=dst, send_sem=disp_send.at[n], recv_sem=disp_recv.at[n],
            device_id={axis: target}, device_id_type=MESH,
        )

    def disp_all(like, n, axis):
        return disp_copy(like, like, n, axis, next_x if axis == "fld" else up)

    to_x = []
    for d in range(1, flds):
        there = lax.rem(fld + d, flds)
        src = part.at[:, pl.ds(pl.multiple_of(there * span, span), span), :]
        to_x.append(disp_copy(src, part_x.at[d - 1], 0, "fld", there))
    answers = levs - 1 - lev + flds - 1 - fld

    @pl.when(answers > 0)
    def _():
        pl.semaphore_wait(answered, answers)

    for copy in to_x:
        copy.start()

    lax.fori_loop(2 * GROUPS - 1, ROLES * GROUPS, step, 0)

    names = [
        pltpu.make_async_remote_copy(
            src_ref=label.at[r], dst_ref=label_in.at[r], send_sem=name_sem.at[0], recv_sem=name_sem.at[1],
            device_id={"horiz": partners[r]}, device_id_type=MESH,
        )
        for r in range(ROLES)
    ]
    for copy in names:
        copy.start()

    def halo(src, dst, n):
        return [
            pltpu.make_async_remote_copy(
                src_ref=src.at[way], dst_ref=dst.at[way], send_sem=halo_send.at[n], recv_sem=halo_recv.at[n],
                device_id={"lev": target}, device_id_type=MESH,
            )
            for way, target in enumerate((down, up))
        ]

    def halo_both(src, dst, n):
        return pltpu.make_async_remote_copy(
            src_ref=src, dst_ref=dst, send_sem=halo_send.at[n], recv_sem=halo_recv.at[n],
            device_id={"lev": up}, device_id_type=MESH,
        )

    slot_halo = halo(slot_edge, slot_edge_in, 0)
    for copy in slot_halo:
        copy.start()

    disp_all(part_x, 0, "fld").wait_recv()
    mine = pl.multiple_of(fld * span, span)
    total = part[:, pl.ds(mine, span), :]
    for d in range(flds - 1):
        total = total + part_x[d]
    whole[:, pl.ds(mine, span), :] = total
    to_y = []
    for d in range(1, levs):
        there = lax.rem(lev + d, levs)
        src = whole.at[:, pl.ds(pl.multiple_of(mine + there * short, short), short), :]
        to_y.append(disp_copy(src, part_y.at[d - 1], 1, "lev", there))
    for copy in to_y:
        copy.start()

    def own(t, carry):
        horizontal(t, t, h_own, tiles)
        return carry

    lax.fori_loop(0, tiles // 2, own, 0, unroll=8)

    disp_all(part_y, 1, "lev").wait()
    piece = pl.multiple_of(mine + lev * short, short)
    total = whole[:, pl.ds(piece, short), :]
    for d in range(levs - 1):
        total = total + part_y[d]
    part[:, pl.ds(piece, short), :] = total
    back_y = []
    disp_all(part_x, 0, "fld").wait_send()
    for d in range(1, levs):
        there = lax.rem(lev + d, levs)
        at = (slice(None), pl.ds(piece, short), slice(None))
        back_y.append(disp_copy(part.at[at], disp_ref.at[at], 2, "lev", there))
    for copy in back_y:
        copy.start()
    disp_ref[:, pl.ds(piece, short), :] = total

    lax.fori_loop(tiles // 2, tiles, own, 0, unroll=8)

    disp_all(part_y, 2, "lev").wait()
    back_x = []
    for d in range(1, flds):
        there = lax.rem(fld + d, flds)
        at = (slice(None), pl.ds(mine, span), slice(None))
        back_x.append(disp_copy(disp_ref.at[at], disp_ref.at[at], 3, "fld", there))
    for copy in back_x:
        copy.start()


    from_below = jnp.where(lev > 0, 1.0, 0.0).astype(F32)
    from_above = jnp.where(lev < levs - 1, 1.0, 0.0).astype(F32)
    halo_both(slot_edge, slot_edge_in, 0).wait_recv()

    edges = ((0, 1, from_below), (nl - 2, 0, from_above))

    def outer(f, low, r):
        n = 2 + f * 2 + (0 if low == 0 else 1)
        piece = (f, pl.ds(low, 2), pl.ds(r * CAP, CAP), slice(None))
        return pltpu.make_async_remote_copy(
            src_ref=snd.at[piece], dst_ref=rcv.at[piece],
            send_sem=z_send, recv_sem=z_recv.at[n],
            device_id={"horiz": partners[r]}, device_id_type=MESH,
        )

    for f in range(nf):
        for low, way, keep in edges:
            for e in range(2):
                snd[f, low + e] = snd[f, low + e] + keep * slot_edge_in[way, f, e]
            for r in range(1, ROLES):
                outer(f, low, r).start()

    half = blocks // 4
    place = here // 2
    kept = jnp.where(lax.rem(place, half) < half // 2, 0, jnp.where(place < half, KEPT_LOW, KEPT_TOP))
    pieces = [(f, low) for f in range(nf) for low, _, _ in edges]
    for n, (f, low) in enumerate(pieces):

        @pl.when(n < len(pieces) - kept)
        def _(f=f, low=low):
            outer(f, low, 0).start()


    def gather_own(i, carry):
        at = pl.ds(pl.multiple_of(i * tiles, tiles), tiles)
        h_own[at, :] = spread(own_hit, h_own[at, :])
        return carry

    lax.fori_loop(0, fl, gather_own, 0, unroll=2)

    def own_vertical(b, carry):
        at = pl.multiple_of(b * 8, 8)
        for f in range(nf):
            values = [h_own[pl.ds(pl.multiple_of((f * nl + l) * tiles + at, 8), 8), :] for l in range(nl)]

            def emit(e, value, f=f):
                if e < 2:
                    own_edge[0, f, e, pl.ds(at, 8), :] = value
                elif e < nl + 2:
                    acc[f, e - 2, pl.ds(at, 8), :] = value
                else:
                    own_edge[1, f, e - nl - 2, pl.ds(at, 8), :] = value

            vertical(values, emit)
        return carry

    lax.fori_loop(0, tiles // 8, own_vertical, 0)
    own_halo = halo(own_edge, own_edge_in, 1)
    for copy in own_halo:
        copy.start()

    def inner_all(role, roles):
        piece = (slice(None), pl.ds(2, nl - 4), pl.ds(role * CAP, roles * CAP))
        return pltpu.make_async_remote_copy(
            src_ref=snd.at[piece], dst_ref=rcv.at[piece], send_sem=z_send, recv_sem=z_recv.at[role],
            device_id={"horiz": pole}, device_id_type=MESH,
        )

    inner_all(0, 1).wait_recv()
    for n, (f, low) in enumerate(pieces):

        @pl.when(n >= len(pieces) - kept)
        def _(f=f, low=low):
            outer(f, low, 0).start()

    halo_both(own_edge, own_edge_in, 1).wait_recv()
    for f in range(nf):
        for low, way, keep in edges:
            for e in range(2):
                acc[f, low + e] = acc[f, low + e] + keep * own_edge_in[way, f, e]

    names_all = pltpu.make_async_remote_copy(
        src_ref=label, dst_ref=label_in, send_sem=name_sem.at[0], recv_sem=name_sem.at[1],
        device_id={"horiz": pole}, device_id_type=MESH,
    )
    names_all.wait_recv()
    slot_lane = lax.broadcasted_iota(jnp.int32, (1, tiles), 1)
    arrived = jnp.where(slot_lane < CAP, label_in[0, 0:1], jnp.where(slot_lane < 2 * CAP, label_in[1, 0:1], label_in[2, 0:1]))
    arrived = jnp.where(slot_lane < SLOTS, arrived, -1)
    hit = jnp.where(jnp.broadcast_to(arrived, square) == row, 1.0, 0.0).astype(BF16)[:, :SLOTS]

    inner_all(1, ROLES - 1).wait_recv()

    def finish(m, carry):
        for f in range(nf):
            acc[f, m] = acc[f, m] + spread(hit, rcv[f, m])
        return carry

    lax.fori_loop(2, nl - 2, finish, 0)

    disp_all(part_x, 3, "fld").wait()
    names_all.wait_send()
    halo_both(slot_edge, slot_edge_in, 0).wait_send()
    halo_both(own_edge, own_edge_in, 1).wait_send()
    for f in range(nf):
        for low, _, _ in edges:
            piece = (f, pl.ds(low, 2))
            pltpu.make_async_remote_copy(
                src_ref=snd.at[piece], dst_ref=rcv.at[piece], send_sem=z_send,
                recv_sem=z_recv.at[2 + f * 2 + (0 if low == 0 else 1)],
                device_id={"horiz": pole}, device_id_type=MESH,
            ).wait_recv()
            for e in range(2):
                acc[f, low + e] = acc[f, low + e] + spread(hit, rcv[f, low + e])
    pltpu.make_async_remote_copy(
        src_ref=snd, dst_ref=rcv, send_sem=z_send, recv_sem=z_recv.at[0],
        device_id={"horiz": pole}, device_id_type=MESH,
    ).wait_send()


def deliver(field_ref, disp_ref, field_out, disp_out, sem):
    copies = [
        pltpu.make_async_copy(field_ref, field_out, sem.at[0]),
        pltpu.make_async_copy(disp_ref, disp_out, sem.at[1]),
    ]
    for copy in copies:
        copy.start()
    for copy in copies:
        copy.wait()


def shards(mesh, adj_out, interp, vert_wts, vert_base, dep_tile, traj_grad):
    nf, nl, tiles, cols = adj_out.shape
    blocks, levs, flds = mesh.shape["horiz"], mesh.shape["lev"], mesh.shape["fld"]
    fl = nf * nl
    span = tiles // flds
    short = span // levs
    hbm = pl.BlockSpec(memory_space=pl.ANY)
    vmem = pl.BlockSpec(memory_space=pltpu.VMEM)
    dma = pltpu.SemaphoreType.DMA
    halo_slots = pltpu.VMEM((2, nf, 2, SLOTS, cols), F32)
    halo_own = pltpu.VMEM((2, nf, 2, tiles, cols), F32)
    field, disp = pl.pallas_call(
        functools.partial(kernel, blocks, levs, flds, nf, nl, tiles),
        out_shape=(
            pltpu.VMEM((nf, nl, tiles, cols), F32),
            pltpu.VMEM((2, tiles, cols), F32),
        ),
        in_specs=[hbm] * 6,
        out_specs=(vmem, vmem),
        scratch_shapes=[
            pltpu.VMEM((fl, tiles, cols), BF16),
            pltpu.VMEM((tiles, cols, cols), BF16),
            pltpu.VMEM((2, fl, tiles, cols), BF16),
            pltpu.VMEM((fl * tiles + tiles, cols), F32),
            pltpu.VMEM((fl * SLOTS + SLOTS, cols), F32),
            pltpu.VMEM((fl * tiles + tiles, cols), F32),
            pltpu.VMEM((nf, nl, SLOTS, cols), F32),
            pltpu.VMEM((nf, nl, SLOTS, cols), F32),
            halo_slots, halo_slots, halo_own, halo_own,
            pltpu.VMEM((1, tiles), jnp.int32),
            pltpu.SMEM((4, nl), F32),
            pltpu.SMEM((nl,), jnp.int32),
            pltpu.VMEM((ROLES, 8, tiles), jnp.int32),
            pltpu.VMEM((ROLES, 8, tiles), jnp.int32),
            pltpu.VMEM((8, tiles), jnp.int32),
            pltpu.SMEM((8, tiles), jnp.int32),
            pltpu.VMEM((2, tiles, cols), F32),
            pltpu.VMEM((flds - 1, 2, span, cols), F32),
            pltpu.VMEM((levs - 1, 2, short, cols), F32),
            pltpu.VMEM((2, tiles, cols), F32),
            dma((5,)), pltpu.SemaphoreType.REGULAR, dma((2,)), dma, dma((2 + 2 * nf,)),
            dma((2,)), dma((2,)), dma((4,)), dma((4,)),
        ],
        compiler_params=pltpu.CompilerParams(
            collective_id=0, has_side_effects=True, vmem_limit_bytes=VMEM_BYTES
        ),
    )(*[
        pltpu.with_memory_space_constraint(x, pltpu.HBM)
        for x in (
            adj_out.reshape(fl, tiles, cols), interp, traj_grad.reshape(2, fl, tiles, cols),
            dep_tile.reshape(1, tiles), vert_wts.T, vert_base,
        )
    ])
    return pl.pallas_call(
        deliver,
        out_shape=(pltpu.HBM(field.shape, F32), pltpu.HBM(disp.shape, F32)),
        in_specs=[vmem] * 2,
        out_specs=(hbm, hbm),
        scratch_shapes=[dma((2,))],
    )(*[pltpu.with_memory_space_constraint(x, pltpu.VMEM) for x in (field, disp)])


def solution(mesh):
    return jax.shard_map(
        functools.partial(shards, mesh),
        mesh=mesh,
        in_specs=(
            P("fld", "lev", "horiz", None),
            P("horiz", None, None),
            P("lev", None),
            P("lev"),
            P("horiz"),
            P(None, "fld", "lev", "horiz", None),
        ),
        out_specs=(P("fld", "lev", "horiz", None), P(None, "horiz", None)),
        check_vma=False,
    )
```
